128 devices in a mesh: fsdp: 32 (over z, x_hi, y), tensor: 4 (over x_lo, core).
Axes of the slice: x: 4 (x_hi: 2, x_lo: 2; x = x_hi * 2 + x_lo), y: 4, z: 4, core: 2. Of those that a mesh axis runs over, the one named last changes fastest.
Arguments:
- tokens: bfloat16 [512, 32, 2048], P('tensor', 'fsdp'), may hold values from -6 to 6
- attend_gain: bfloat16 [2048], P('fsdp'), may hold values from 0.5 to 1.5
- joint_weight: bfloat16 [2048, 4096], P('fsdp', 'tensor'), may hold values from -0.125 to 0.125
- mixing_weight: bfloat16 [2048, 2048], P('tensor', 'fsdp'), may hold values from -0.75 to 0.75
- feed_gain: bfloat16 [2048], P('fsdp'), may hold values from 0.5 to 1.5
- gate_weight: bfloat16 [2048, 8192], P('fsdp', 'tensor'), may hold values from -0.125 to 0.125
- up_weight: bfloat16 [2048, 8192], P('fsdp', 'tensor'), may hold values from -0.125 to 0.125
- down_weight: bfloat16 [8192, 2048], P('tensor', 'fsdp'), may hold values from -0.0625 to 0.0625
- lengths: int32 [32, 7], P('fsdp'), may hold values from 1 to 256, 512 in all within a row
- parents: int32 [32, 7], P('fsdp'), may hold values from 0 to 5, as said below
- cotangent: float32 [512, 32, 2048], P('tensor', 'fsdp'), may hold values from -6 to 6
Outputs:
- layer_output: float32 [512, 32, 2048], P('tensor', 'fsdp')
- input_gradient: float32 [512, 32, 2048], P('tensor', 'fsdp')
- attend_gradient: float32 [2048], P('fsdp')
- joint_gradient: float32 [2048, 4096], P('fsdp', 'tensor')
- mixing_gradient: float32 [2048, 2048], P('tensor', 'fsdp')
- feed_gradient: float32 [2048], P('fsdp')
- gate_gradient: float32 [2048, 8192], P('fsdp', 'tensor')
- up_gradient: float32 [2048, 8192], P('fsdp', 'tensor')
- down_gradient: float32 [8192, 2048], P('tensor', 'fsdp')
The draws below stay inside these ranges and needn't reach their ends.
Inputs may be any that keep to these rules, and one draw needn't show every extreme that they name: `lengths`: each row sums to 512, and every row's largest entry is 256. `parents`: entry s >= 1 of a row is a segment number below s; entry 0 is 0.
All inputs are finite; a program needn't handle non-finite values.
Results may differ from the reference program's by a relative error of at most 0.028.
Values may be sent and summed in bfloat16 or wider, within the bound.
No kernel may reach another device: no remote copies, remote signals or barrier semaphores. Data moves between devices by JAX's collectives and lax.ppermute only.
A program may use at most 192 MiB of HBM per device.

```python
import math
import jax
import jax.numpy as jnp
import numpy as np
from jax import lax

D = 2048
HEADS = 16
KVH = 8
HD = 128
FF = 8192
TREE_LEN = 512
NSEG = 7
MOST = 256
TREES = 32
JOINT = 4096


def draw_parents(key, part):
    key = jax.random.fold_in(key, 7)
    order = jnp.arange(NSEG, dtype=jnp.int32)
    tree_index = jnp.arange(TREES, dtype=jnp.int32)
    raw = jax.random.randint(key, (TREES, NSEG), 0, 1048576, dtype=jnp.int32)
    picked = jnp.where(order > 0, raw % jnp.maximum(order, 1), 0).astype(jnp.int32)
    corner = (tree_index[:, None] == 0) & (order[None, :] == NSEG - 1)
    return jnp.where(corner, NSEG - 2, picked).astype(jnp.int32)


def with_spikes(drawn, rng, source, target, blocks, factor):
    def block_of(dim):
        return (jnp.arange(drawn.shape[dim]) // (drawn.shape[dim] // blocks)).reshape((-1,) + (1,) * (drawn.ndim - 1 - dim))

    one_side = jax.random.permutation(rng, blocks)[block_of(target)]
    other_side = (block_of(target) + blocks // 2) % blocks
    return jnp.where((block_of(source) == one_side) | (block_of(source) == other_side), factor * drawn, drawn)


def levels(stream_key, dims, shards, smallest, top_value):
    factor_of = 1.0
    for dim, shards_of in shards:
        steps = jax.random.uniform(jax.random.fold_in(jax.random.fold_in(stream_key, 6), dim), (shards_of,), jnp.float32, smallest / len(shards), top_value / len(shards))
        factor_of = factor_of * jnp.repeat(jnp.exp(steps), dims[dim] // shards_of).reshape((-1,) + (1,) * (len(dims) - 1 - dim))
    return factor_of


def profile(number_of, total, most, skew):
    loads = [(1 << 20) // math.isqrt(grade ** skew) + 1 for grade in range(2, number_of + 1)]
    rest, given = total - most - (number_of - 1), [1] * (number_of - 1)
    while rest > 0:
        movable = [i for i in range(number_of - 1) if given[i] < most]
        mass, remaining = sum([loads[i] for i in movable]), rest
        for i in movable:
            more = min(most - given[i], max(1, remaining * loads[i] // mass), rest)
            given[i] = given[i] + more
            rest = rest - more
    return np.array([most] + given)


def ragged_sizes(own_key, number_of, total, bound, skew):
    if number_of == 2:
        one = jax.random.randint(own_key, (), max(1, total - bound), min(bound, total - 1) + 1)
        return jnp.stack([one, total - one])
    tallies = jnp.asarray(profile(number_of, total, bound, skew), jnp.int32)
    couples = (number_of - 1) // 2
    giver, receiver = tallies[1:1 + 2 * couples:2], tallies[2:2 + 2 * couples:2]
    room = jnp.minimum(giver - 1, bound - receiver)
    passed = jax.random.randint(jax.random.fold_in(own_key, 1), (couples,), 0, 1 << 20) % (room + 1)
    tallies = tallies.at[1:1 + 2 * couples:2].set(giver - passed).at[2:2 + 2 * couples:2].set(receiver + passed)
    return tallies[jax.random.permutation(jax.random.fold_in(own_key, 2), number_of)]


def noise(own_key, extent, scale, bound, split=(), held_as=jnp.bfloat16):
    values = jax.random.normal(own_key, extent, jnp.float32) * scale
    if len(split) > 0:
        values = levels(own_key, extent, split, -0.22, 0.18) * values
    return jnp.clip(values, min=-bound, max=bound).astype(held_as)


def bell_draw_with(key, shape, deviation, bound, cuts, heavy, kind=jnp.bfloat16):
    drawn = deviation * jax.random.normal(key, shape, jnp.float32)
    if cuts:
        drawn = drawn * levels(key, shape, cuts, -0.22, 0.18)
    return jnp.clip(with_spikes(drawn, jax.random.fold_in(key, 3), *heavy), -bound, bound).astype(kind)


def setup_inputs(seed: int = 0) -> dict:
    seeds = jax.random.split(jax.random.key(seed), 12)
    return {
        "tokens": noise(seeds[0], (TREE_LEN, TREES, D), 1.0, 6.0, ((0, 4), (1, 32))),
        "attend_gain": jnp.clip(1.0 + 0.1 * jax.random.normal(seeds[1], (D,), jnp.float32), 0.5, 1.5).astype(jnp.bfloat16),
        "joint_weight": noise(seeds[2], (D, JOINT), D ** -0.5, 0.125, ((0, 32), (1, 4))),
        "mixing_weight": noise(seeds[3], (HEADS * HD, D), (HEADS * HD // 32) ** -0.5, 0.75, ((0, 4), (1, 32))),
        "feed_gain": jnp.clip(1.0 + 0.1 * jax.random.normal(seeds[4], (D,), jnp.float32), 0.5, 1.5).astype(jnp.bfloat16),
        "gate_weight": noise(seeds[5], (D, FF), D ** -0.5, 0.125, ((0, 32), (1, 4))),
        "up_weight": noise(seeds[6], (D, FF), D ** -0.5, 0.125, ((0, 32), (1, 4))),
        "down_weight": noise(seeds[7], (FF, D), FF ** -0.5, 0.0625, ((0, 4), (1, 32))),
        "lengths": jax.vmap(lambda own: ragged_sizes(own, NSEG, TREE_LEN, MOST, 2))(jax.random.split(seeds[8], TREES)).reshape((TREES, NSEG)).astype(jnp.int32),
        "parents": draw_parents(jax.random.fold_in(seeds[11], 71), 0),
        "cotangent": bell_draw_with(seeds[10], (TREE_LEN, TREES, D), 1.0, 6.0, ((0, 4), (1, 32)), (1, 2, 32, 2.75), jnp.float32),
    }


EPSILON = 1e-06
ROPE_BASE = 1000000.0
NEGATIVE = -1e+30

@jax.custom_vjp
def low(v):
    return lax.optimization_barrier(v.astype(jnp.bfloat16)).astype(jnp.float32)

@jax.custom_vjp
def low_back(v):
    return v

def low_keep(v):
    return (low(v), None)

def low_pass(kept, grad):
    return (grad,)

def back_keep(v):
    return (v, None)

def back_low(kept, grad):
    return (low(grad),)
low.defvjp(low_keep, low_pass)
low_back.defvjp(back_keep, back_low)

def tree_layout(lengths, parents, count):
    nseg = lengths.shape[1]
    batch = lengths.shape[0]
    ends = jnp.cumsum(lengths, axis=1).astype(jnp.int32)
    starts = ends - lengths
    place = jnp.arange(count, dtype=jnp.int32)
    segment = lax.optimization_barrier(jnp.sum((place[:, None, None] >= ends[None, :, :nseg - 1]).astype(jnp.int32), axis=2))
    order = jnp.arange(nseg, dtype=jnp.int32)
    rows = [(order == 0).astype(jnp.float32)[None, :] * jnp.ones((batch, 1), jnp.float32)]
    depth = [jnp.zeros((batch,), jnp.int32)]
    for later in range(1, nseg):
        above = jnp.zeros_like(rows[0])
        reach = jnp.zeros_like(depth[0])
        for earlier in range(later):
            hit = parents[:, later] == earlier
            above = above + hit.astype(jnp.float32)[:, None] * rows[earlier]
            reach = reach + jnp.where(hit, depth[earlier] + lengths[:, earlier], 0).astype(jnp.int32)
        rows.append(above + (order == later).astype(jnp.float32)[None, :])
        depth.append(reach)
    ancestry = jnp.stack(rows, axis=1)
    begin = jnp.stack(depth, axis=1)
    pick = (segment[:, :, None] == order[None, None, :]).astype(jnp.float32)
    shift = (begin - starts).astype(jnp.float32)
    position = place[:, None].astype(jnp.float32) + lax.optimization_barrier(jnp.sum(pick * shift[None], axis=2))
    linked = jnp.einsum('ibs,bst,jbt->bij', pick, ancestry, pick)
    causal = place[None, :] <= place[:, None]
    return (position, (linked > 0.5) & causal[None])

def rotary_tables(position, width):
    half = width // 2
    rates = jnp.exp(jnp.arange(half, dtype=jnp.float32) * (-2.0 * math.log(ROPE_BASE) / width))
    angle = position[..., None] * rates
    return (jnp.cos(angle), jnp.sin(angle))

def rotate(values, cosine, sine):
    half = values.shape[-1] // 2
    shape = cosine.shape[:-1] + (1,) * (values.ndim - cosine.ndim) + cosine.shape[-1:]
    cosine = cosine.reshape(shape)
    sine = sine.reshape(shape)
    first = values[..., :half]
    second = values[..., half:]
    return jnp.concatenate([first * cosine - second * sine, second * cosine + first * sine], axis=-1)

def matmul(left, right):
    return jnp.dot(left, right, precision=lax.Precision.HIGHEST, preferred_element_type=jnp.float32)

def forward(incoming, weights, cosine, sine, allowed):
    attend_gain, joint_weight, mixing_weight, feed_gain, gate_weight, up_weight, down_weight = weights
    count = incoming.shape[0]
    groups = HEADS // KVH
    scale_one = lax.rsqrt(lax.optimization_barrier(jnp.mean(incoming * incoming, axis=1, keepdims=True)) + EPSILON)
    normed_one = low(incoming * scale_one * attend_gain)
    joint = low_back(matmul(normed_one, joint_weight)).reshape(count, KVH, groups + 2, HD)
    queries = low(rotate(joint[:, :, :groups], cosine, sine))
    keys = low(rotate(joint[:, :, groups], cosine, sine))
    values = low(joint[:, :, groups + 1])
    scores = low_back(jnp.einsum('ikgd,jkd->kgij', queries, keys, precision=lax.Precision.HIGHEST) * (1.0 / math.sqrt(HD)))
    masked = jnp.where(allowed, scores, NEGATIVE)
    highest = lax.optimization_barrier(jnp.max(masked, axis=-1, keepdims=True))
    powers = jnp.exp(masked - highest)
    chance = powers / lax.optimization_barrier(jnp.sum(powers, axis=-1, keepdims=True))
    mixed = jnp.einsum('kgij,jkd->ikgd', low(chance), values, precision=lax.Precision.HIGHEST)
    mixed = low(low_back(mixed)).reshape(count, HEADS * HD)
    middle = incoming + low_back(matmul(mixed, mixing_weight))
    scale_two = lax.rsqrt(lax.optimization_barrier(jnp.mean(middle * middle, axis=1, keepdims=True)) + EPSILON)
    normed_two = low(middle * scale_two * feed_gain)
    gate = low_back(matmul(normed_two, gate_weight))
    upper = low_back(matmul(normed_two, up_weight))
    hidden = low(jax.nn.silu(gate) * upper)
    return middle + low_back(matmul(hidden, down_weight))

def reference(tokens, attend_gain, joint_weight, mixing_weight, feed_gain, gate_weight, up_weight, down_weight, lengths, parents, cotangent):
    params = tuple((item.astype(jnp.float32) for item in (attend_gain, joint_weight, mixing_weight, feed_gain, gate_weight, up_weight, down_weight)))

    def one_tree(sums, item):
        column, slope, sizes, links = item
        position, allowed = tree_layout(sizes[None], links[None], TREE_LEN)
        cosine, sine = rotary_tables(position[:, 0], HD)

        def run(incoming, *weights):
            return forward(incoming, weights, cosine, sine, allowed[0])
        result, pullback = jax.vjp(run, column.astype(jnp.float32), *params)
        grads = pullback(slope.astype(jnp.float32))
        sums = tuple((total + grad for total, grad in zip(sums, grads[1:])))
        return (sums, (result, grads[0]))
    zeros = tuple((jnp.zeros_like(item) for item in params))
    sums, (results, slopes) = lax.scan(one_tree, zeros, (jnp.swapaxes(tokens, 0, 1), jnp.swapaxes(cotangent, 0, 1), lengths, parents))
    return (jnp.swapaxes(results, 0, 1), jnp.swapaxes(slopes, 0, 1), sums[0], sums[1], sums[2], sums[3], sums[4], sums[5], sums[6])
```

```python
import math

import jax
import jax.numpy as jnp
from jax import lax
from jax.experimental import pallas as pl
from jax.experimental.pallas import tpu as pltpu
from jax.sharding import Mesh
from jax.sharding import PartitionSpec as P

HEADS = 16
KVH = 8
HD = 128
EPSILON = 1e-06
ROPE_BASE = 1000000.0
NEGATIVE = -1e30
MIB = 1024 * 1024

TEAM = ("xh", "xl", "core")
GRID = ("z", "y")

bf16 = jnp.bfloat16
f32 = jnp.float32


def team_swap(value, a, b, c):
    flip = a * 4 + b * 2 + c
    return lax.ppermute(value, TEAM, [(i, i ^ flip) for i in range(8)])


def axis_swap(value, axis, flip):
    return lax.ppermute(value, axis, [(i, i ^ flip) for i in range(4)])


def team_gather(own):
    half = own.shape[0] // 2
    near = team_swap(own, 0, 1, 0)
    next_ = team_swap(own, 1, 1, 0)
    mate = team_swap(own, 0, 0, 1)
    low = team_swap(near[:half], 1, 1, 0)
    high = team_swap(next_[half:], 0, 1, 0)
    near_mate = team_swap(near, 0, 0, 1)
    next_mate = team_swap(next_, 0, 0, 1)
    low_mate = team_swap(low, 0, 0, 1)
    high_mate = team_swap(high, 0, 0, 1)
    return jnp.concatenate(
        [own, mate, near, near_mate, low, high, low_mate, high_mate, next_, next_mate], axis=0
    )


def team_scatter(keep, send):
    got = team_swap(send, 0, 0, 1)
    here = keep[0, 0].astype(f32) + got[0, 0].astype(f32)

    def outgoing(a, b):
        return (keep[a, b].astype(f32) + got[a, b].astype(f32)).astype(bf16)

    near = team_swap(outgoing(0, 1), 0, 1, 0)
    next_ = team_swap(outgoing(1, 1), 1, 1, 0)
    far = team_swap(outgoing(1, 0), 1, 0, 0)
    return here + near.astype(f32) + next_.astype(f32) + far.astype(f32)


def grid_gather(block):
    half = block.shape[1] // 2
    left, right = block[:, :half], block[:, half:]
    left = jnp.concatenate([left] + [axis_swap(left, "y", k) for k in (1, 2, 3)], axis=0)
    right = jnp.concatenate([right] + [axis_swap(right, "z", k) for k in (1, 2, 3)], axis=0)
    return (
        [left] + [axis_swap(left, "z", k) for k in (1, 2, 3)],
        [right] + [axis_swap(right, "y", k) for k in (1, 2, 3)],
    )


def grid_scatter(left, right):
    def one(parts, first, second):
        got = [axis_swap(parts[k], first, k) for k in (1, 2, 3)]
        total = parts[0].astype(f32)
        for item in got:
            total = total + item.astype(f32)
        low = total.astype(bf16)
        got = [axis_swap(low[k], second, k) for k in (1, 2, 3)]
        out = total[0]
        for item in got:
            out = out + item.astype(f32)
        return out

    return jnp.concatenate([one(left, "z", "y"), one(right, "y", "z")], axis=1)


def gather_gains(pair, xh):
    other = team_swap(pair, 1, 0, 0)
    both = jnp.concatenate([jnp.where(xh == 0, pair, other), jnp.where(xh == 0, other, pair)], axis=0)

    def ordered(own, axis):
        me = lax.axis_index(axis)
        got = [own] + [axis_swap(own, axis, k) for k in (1, 2, 3)]
        return jnp.stack([lax.select_n(me ^ k, *got) for k in range(4)])

    whole = ordered(ordered(both, "y"), "z").reshape(32, 128)
    return whole[:, :64].reshape(1, 2048), whole[:, 64:].reshape(1, 2048)


def lane_order(value):
    parts = []
    for z in range(4):
        for y in range(4):
            for xh in range(2):
                start = z * 512 + xh * 256 + y * 64
                parts.append(value[:, start : start + 64])
    return jnp.concatenate(parts, axis=1)


def lane_back(value):
    parts = []
    for z in range(4):
        for xh in range(2):
            for y in range(4):
                start = z * 512 + y * 128 + xh * 64
                parts.append(value[:, start : start + 64])
    return jnp.concatenate(parts, axis=1)


def reorder_kernel(tokens_ref, slope_ref, tokens_out, slope_out, low_out):
    tokens_out[...] = lane_order(tokens_ref[...].astype(f32)).astype(bf16)
    slope = lane_order(slope_ref[...])
    slope_out[...] = slope
    low_out[...] = slope.astype(bf16)


def reorder(tokens, slope):
    shape = tokens.shape
    return pl.pallas_call(
        reorder_kernel,
        out_shape=(
            jax.ShapeDtypeStruct(shape, bf16),
            jax.ShapeDtypeStruct(shape, f32),
            jax.ShapeDtypeStruct(shape, bf16),
        ),
        compiler_params=pltpu.CompilerParams(vmem_limit_bytes=32 * MIB),
    )(tokens, slope)


def tree_tables(lengths, parents, place):
    nseg = lengths.shape[1]
    batch = lengths.shape[0]
    ends = jnp.cumsum(lengths, axis=1)
    starts = ends - lengths
    segment = jnp.sum((place[None, :, None] >= ends[:, None, : nseg - 1]).astype(jnp.int32), axis=2)
    order = jnp.arange(nseg, dtype=jnp.int32)
    rows = [(order == 0).astype(f32)[None, :] * jnp.ones((batch, 1), f32)]
    depth = [jnp.zeros((batch,), jnp.int32)]
    for later in range(1, nseg):
        above = jnp.zeros_like(rows[0])
        reach = jnp.zeros_like(depth[0])
        for earlier in range(later):
            hit = parents[:, later] == earlier
            above = above + hit.astype(f32)[:, None] * rows[earlier]
            reach = reach + jnp.where(hit, depth[earlier] + lengths[:, earlier], 0)
        rows.append(above + (order == later).astype(f32)[None, :])
        depth.append(reach)
    ancestry = jnp.stack(rows, axis=1)
    begin = jnp.stack(depth, axis=1)
    pick = (segment[:, :, None] == order[None, None, :]).astype(f32)
    shift = (begin - starts).astype(f32)
    position = place[None, :].astype(f32) + jnp.sum(pick * shift[:, None, :], axis=2)
    linked = jnp.einsum("bis,bst,bjt->bij", pick, ancestry, pick)
    causal = place[None, :] <= place[:, None]
    return position, ((linked > 0.5) & causal[None]).astype(bf16)


def rotary_tables(position):
    half = HD // 2
    rates = jnp.exp(jnp.arange(half, dtype=f32) * (-2.0 * math.log(ROPE_BASE) / HD))
    angle = position[..., None] * rates
    cosine, sine = jnp.cos(angle), jnp.sin(angle)
    return jnp.concatenate([cosine, cosine], axis=-1), jnp.concatenate([-sine, sine], axis=-1)


def dot(left, right, contract):
    return lax.dot_general(
        left, right, (((contract[0],), (contract[1],)), ((), ())), preferred_element_type=f32
    )


def turn(value, cosine, sine):
    return value * cosine + pltpu.roll(value, HD // 2, 1) * sine


def attend_kernel(
    me_ref, n_ref, l0, l1, l2, l3, r0, r1, r2, r3, cos_ref, sin_ref, mask_ref,
    w_ref, qkv_ref, mixed_ref, keep_ref, send_ref,
):
    z, y = me_ref[0], me_ref[1]

    @pl.when(pl.program_id(0) == 0)
    def _():
        for dz, (left, right) in enumerate(((l0, r0), (l1, r1), (l2, r2), (l3, r3))):
            for dy in range(4):
                first = pl.multiple_of(((z ^ dz) * 4 + (y ^ dy)) * 128, 128)
                w_ref[pl.ds(first, 128), 0:384] = left[dy * 128 : dy * 128 + 128, :]
                second = pl.multiple_of(((z ^ dy) * 4 + (y ^ dz)) * 128, 128)
                w_ref[pl.ds(second, 128), 384:768] = right[dy * 128 : dy * 128 + 128, :]

    joint = dot(n_ref[...], w_ref[:, 0:512], (1, 0))
    cosine, sine = cos_ref[0], sin_ref[0]
    keys = turn(joint[:, 256:384], cosine, sine).astype(bf16)
    values = joint[:, 384:512].astype(bf16)
    qkv_ref[:, 256:384] = keys
    qkv_ref[:, 384:512] = values
    allowed = mask_ref[0].astype(f32) > 0.5
    for head in range(2):
        at = slice(head * HD, head * HD + HD)
        queries = turn(joint[:, at], cosine, sine).astype(bf16)
        qkv_ref[:, at] = queries
        scores = dot(queries, keys, (1, 1)) * (1.0 / math.sqrt(HD))
        scores = jnp.where(allowed, scores, NEGATIVE)
        powers = jnp.exp(scores - jnp.max(scores, axis=1, keepdims=True))
        chance = (powers / jnp.sum(powers, axis=1, keepdims=True)).astype(bf16)
        mixed_ref[:, at] = dot(chance, values, (1, 0)).astype(bf16)
    part = dot(mixed_ref[...], w_ref[:, 512:768], (1, 1)).astype(bf16)
    for b in range(2):
        keep_ref[0, b] = part[b * 256 : b * 256 + 128, :]
        send_ref[0, b] = part[b * 256 + 128 : b * 256 + 256, :]


def attend(me, normed, left, right, cosine, sine, mask):
    whole = lambda shape: pl.BlockSpec(shape, lambda i, me: (0,) * len(shape))
    tree = lambda width: pl.BlockSpec((512, width), lambda i, me: (i, 0))
    table = lambda width: pl.BlockSpec((1, 512, width), lambda i, me: (i, 0, 0))
    quarter = pl.BlockSpec((1, 2, 128, 2048), lambda i, me: (i, 0, 0, 0))
    return pl.pallas_call(
        attend_kernel,
        grid_spec=pltpu.PrefetchScalarGridSpec(
            num_scalar_prefetch=1,
            grid=(2,),
            in_specs=[tree(2048)] + [whole((512, 384))] * 8 + [table(HD), table(HD), table(512)],
            out_specs=[whole((2048, 768)), tree(512), tree(256), quarter, quarter],
        ),
        out_shape=(
            jax.ShapeDtypeStruct((2048, 768), bf16),
            jax.ShapeDtypeStruct((1024, 512), bf16),
            jax.ShapeDtypeStruct((1024, 256), bf16),
            jax.ShapeDtypeStruct((2, 2, 128, 2048), bf16),
            jax.ShapeDtypeStruct((2, 2, 128, 2048), bf16),
        ),
        compiler_params=pltpu.CompilerParams(vmem_limit_bytes=56 * MIB),
        cost_estimate=pl.CostEstimate(
            flops=4 * 1024 * 2048 * 384, bytes_accessed=24 * MIB, transcendentals=1 << 20
        ),
    )(me, normed, *left, *right, cosine, sine, mask)


def attend_back_kernel(
    me_ref, branch_ref, n_ref, w_ref, qkv_ref, mixed_ref, cos_ref, sin_ref, mask_ref,
    left_ref, right_ref, keep_ref, send_ref, js_ref, joint_acc, mixing_acc,
):
    z, y = me_ref[0], me_ref[1]
    step = pl.program_id(0)
    factor = 1.0 / math.sqrt(HD)
    mixed_slope = dot(branch_ref[...], w_ref[:, 512:768], (1, 0)).astype(bf16)
    cosine, sine = cos_ref[0], -sin_ref[0]
    allowed = mask_ref[0].astype(f32) > 0.5
    keys = qkv_ref[:, 256:384]
    values = qkv_ref[:, 384:512]
    key_slope = jnp.zeros((512, HD), f32)
    value_slope = jnp.zeros((512, HD), f32)
    for head in range(2):
        at = slice(head * HD, head * HD + HD)
        queries = qkv_ref[:, at]
        scores = jnp.where(allowed, dot(queries, keys, (1, 1)) * factor, NEGATIVE)
        powers = jnp.exp(scores - jnp.max(scores, axis=1, keepdims=True))
        chance = powers / jnp.sum(powers, axis=1, keepdims=True)
        slope = mixed_slope[:, at]
        value_slope += dot(chance.astype(bf16), slope, (0, 0))
        chance_slope = dot(slope, values, (1, 1))
        balance = jnp.sum(chance * chance_slope, axis=1, keepdims=True)
        score_slope = (chance * (chance_slope - balance)).astype(bf16)
        query_slope = dot(score_slope, keys, (1, 0)) * factor
        js_ref[:, at] = turn(query_slope, cosine, sine).astype(bf16)
        key_slope += dot(score_slope, queries, (0, 0)) * factor
    js_ref[:, 256:384] = turn(key_slope, cosine, sine).astype(bf16)
    js_ref[:, 384:512] = value_slope.astype(bf16)
    joint_slope = js_ref[...]
    joint_part = dot(n_ref[...], joint_slope, (0, 0))
    mixing_part = dot(branch_ref[...], mixed_ref[...], (0, 0))

    @pl.when(step == 0)
    def _():
        joint_acc[...] = joint_part
        mixing_acc[...] = mixing_part

    @pl.when(step == 1)
    def _():
        joint_acc[...] += joint_part
        mixing_acc[...] += mixing_part
        for k in range(4):
            for j in range(4):
                first = pl.multiple_of(((z ^ k) * 4 + (y ^ j)) * 128, 128)
                left_ref[k, j] = joint_acc[pl.ds(first, 128), 0:384].astype(bf16)
                second = pl.multiple_of(((z ^ j) * 4 + (y ^ k)) * 128, 128)
                right_ref[k, j, :, 0:128] = joint_acc[pl.ds(second, 128), 384:512].astype(bf16)
                right_ref[k, j, :, 128:384] = mixing_acc[pl.ds(second, 128), :].astype(bf16)

    part = dot(joint_slope, w_ref[:, 0:512], (1, 1)).astype(bf16)
    for b in range(2):
        keep_ref[0, b] = part[b * 256 : b * 256 + 128, :]
        send_ref[0, b] = part[b * 256 + 128 : b * 256 + 256, :]


def attend_back(me, branch, normed, weights, qkv, mixed, cosine, sine, mask):
    whole = lambda shape: pl.BlockSpec(shape, lambda i, me: (0,) * len(shape))
    tree = lambda width: pl.BlockSpec((512, width), lambda i, me: (i, 0))
    table = lambda width: pl.BlockSpec((1, 512, width), lambda i, me: (i, 0, 0))
    quarter = pl.BlockSpec((1, 2, 128, 2048), lambda i, me: (i, 0, 0, 0))
    return pl.pallas_call(
        attend_back_kernel,
        grid_spec=pltpu.PrefetchScalarGridSpec(
            num_scalar_prefetch=1,
            grid=(2,),
            in_specs=[
                tree(2048), tree(2048), whole((2048, 768)), tree(512), tree(256),
                table(HD), table(HD), table(512),
            ],
            out_specs=[whole((4, 4, 128, 384)), whole((4, 4, 128, 384)), quarter, quarter],
            scratch_shapes=[
                pltpu.VMEM((512, 512), bf16),
                pltpu.VMEM((2048, 512), f32),
                pltpu.VMEM((2048, 256), f32),
            ],
        ),
        out_shape=(
            jax.ShapeDtypeStruct((4, 4, 128, 384), bf16),
            jax.ShapeDtypeStruct((4, 4, 128, 384), bf16),
            jax.ShapeDtypeStruct((2, 2, 128, 2048), bf16),
            jax.ShapeDtypeStruct((2, 2, 128, 2048), bf16),
        ),
        compiler_params=pltpu.CompilerParams(vmem_limit_bytes=56 * MIB),
        cost_estimate=pl.CostEstimate(
            flops=6 * 1024 * 2048 * 512, bytes_accessed=24 * MIB, transcendentals=1 << 20
        ),
    )(me, branch, normed, weights, qkv, mixed, cosine, sine, mask)


def hidden_slope_kernel(x_ref, w_ref, o_ref):
    o_ref[...] = dot(x_ref[...], w_ref[...], (1, 0))


def hidden_slopes(feed, weights):
    return pl.pallas_call(
        hidden_slope_kernel,
        grid=(4,),
        in_specs=[
            pl.BlockSpec((1024, 2048), lambda j: (0, 0)),
            pl.BlockSpec((2048, 256), lambda j: (0, j + 8)),
        ],
        out_specs=pl.BlockSpec((1024, 256), lambda j: (0, j)),
        out_shape=jax.ShapeDtypeStruct((1024, 1024), f32),
        compiler_params=pltpu.CompilerParams(vmem_limit_bytes=48 * MIB),
        cost_estimate=pl.CostEstimate(
            flops=2 * 1024 * 2048 * 1024, bytes_accessed=12 * MIB, transcendentals=0
        ),
    )(feed, weights)


def feed_kernel(n_ref, gate_ref, up_ref, slope_ref, out_ref):
    gate = dot(n_ref[...], gate_ref[...], (1, 0))
    upper = dot(n_ref[...], up_ref[...], (1, 0))
    slope = slope_ref[...]
    sigma = jax.nn.sigmoid(gate)
    active = gate * sigma
    out_ref[0] = (slope * upper * sigma * (1.0 + gate * (1.0 - sigma))).astype(bf16)
    out_ref[1] = (slope * active).astype(bf16)
    out_ref[2] = (active * upper).astype(bf16)


def feed_forward(normed, weights, slopes):
    return pl.pallas_call(
        feed_kernel,
        grid=(4,),
        in_specs=[
            pl.BlockSpec((1024, 2048), lambda j: (0, 0)),
            pl.BlockSpec((2048, 256), lambda j: (0, j)),
            pl.BlockSpec((2048, 256), lambda j: (0, j + 4)),
            pl.BlockSpec((1024, 256), lambda j: (0, j)),
        ],
        out_specs=pl.BlockSpec((3, 1024, 256), lambda j: (0, 0, j)),
        out_shape=jax.ShapeDtypeStruct((3, 1024, 1024), bf16),
        compiler_params=pltpu.CompilerParams(vmem_limit_bytes=48 * MIB),
        cost_estimate=pl.CostEstimate(
            flops=4 * 1024 * 2048 * 1024, bytes_accessed=22 * MIB, transcendentals=1 << 20
        ),
    )(normed, weights, weights, slopes)


def feed_grad_kernel(n_ref, f_ref, s_ref, out_ref, turned):
    step = pl.program_id(0)

    @pl.when(step == 0)
    def _():
        turned[...] = n_ref[...].T

    @pl.when(step == 8)
    def _():
        turned[...] = f_ref[...].T

    out_ref[...] = dot(turned[...], s_ref[0], (1, 0)).astype(bf16)


def feed_grads(normed, feed, slopes):
    return pl.pallas_call(
        feed_grad_kernel,
        grid=(12,),
        in_specs=[
            pl.BlockSpec((1024, 2048), lambda j: (0, 0)),
            pl.BlockSpec((1024, 2048), lambda j: (0, 0)),
            pl.BlockSpec((1, 1024, 256), lambda j: (j // 4, 0, j % 4)),
        ],
        out_specs=pl.BlockSpec((2048, 256), lambda j: (0, j)),
        out_shape=jax.ShapeDtypeStruct((2048, 3072), bf16),
        scratch_shapes=[pltpu.VMEM((2048, 1024), bf16)],
        compiler_params=pltpu.CompilerParams(vmem_limit_bytes=48 * MIB),
        cost_estimate=pl.CostEstimate(
            flops=6 * 1024 * 2048 * 1024, bytes_accessed=26 * MIB, transcendentals=0
        ),
    )(normed, feed, slopes)


def split_rows(part, keep_ref, send_ref):
    for a in range(2):
        for b in range(2):
            first = a * 512 + b * 256
            keep_ref[a, b] = part[first : first + 128, :]
            send_ref[a, b] = part[first + 128 : first + 256, :]


def normed_slope_kernel(g_ref, u_ref, wg_ref, wu_ref, keep_ref, send_ref):
    part = dot(g_ref[0], wg_ref[...], (1, 1)) + dot(u_ref[0], wu_ref[...], (1, 1))
    split_rows(part.astype(bf16), keep_ref, send_ref)


def normed_slopes(slopes, weights):
    half = jax.ShapeDtypeStruct((2, 2, 128, 2048), bf16)
    return pl.pallas_call(
        normed_slope_kernel,
        grid=(8,),
        in_specs=[
            pl.BlockSpec((1, 1024, 1024), lambda j: (0, 0, 0)),
            pl.BlockSpec((1, 1024, 1024), lambda j: (1, 0, 0)),
            pl.BlockSpec((256, 1024), lambda j: (j, 0)),
            pl.BlockSpec((256, 1024), lambda j: (j, 1)),
        ],
        out_specs=[pl.BlockSpec((2, 2, 128, 256), lambda j: (0, 0, 0, j))] * 2,
        out_shape=(half, half),
        compiler_params=pltpu.CompilerParams(vmem_limit_bytes=48 * MIB),
        cost_estimate=pl.CostEstimate(
            flops=4 * 1024 * 2048 * 1024, bytes_accessed=16 * MIB, transcendentals=0
        ),
    )(slopes, slopes, weights, weights)


def down_kernel(h_ref, w_ref, keep_ref, send_ref):
    split_rows(dot(h_ref[0], w_ref[...], (1, 1)).astype(bf16), keep_ref, send_ref)


def down(slopes, weights):
    half = jax.ShapeDtypeStruct((2, 2, 128, 2048), bf16)
    return pl.pallas_call(
        down_kernel,
        grid=(8,),
        in_specs=[
            pl.BlockSpec((1, 1024, 1024), lambda j: (2, 0, 0)),
            pl.BlockSpec((256, 1024), lambda j: (j, 2)),
        ],
        out_specs=[pl.BlockSpec((2, 2, 128, 256), lambda j: (0, 0, 0, j))] * 2,
        out_shape=(half, half),
        compiler_params=pltpu.CompilerParams(vmem_limit_bytes=48 * MIB),
        cost_estimate=pl.CostEstimate(
            flops=2 * 1024 * 2048 * 1024, bytes_accessed=10 * MIB, transcendentals=0
        ),
    )(slopes, weights)


def norm_back(slope, incoming, scale, gain):
    weighted = slope * gain
    cubed = scale * scale * scale
    return scale * weighted - incoming * cubed * jnp.mean(weighted * incoming, axis=1, keepdims=True)


def shards(
    tokens, attend_gain, joint_weight, mixing_weight, feed_gain, gate_weight, up_weight,
    down_weight, lengths, parents, cotangent,
):
    z, y = lax.axis_index("z"), lax.axis_index("y")
    xh, xl, core = lax.axis_index("xh"), lax.axis_index("xl"), lax.axis_index("core")
    me = jnp.stack([z, y]).astype(jnp.int32)

    def both_rows(own, other):
        return jnp.concatenate(
            [jnp.where(xh == 0, own, other), jnp.where(xh == 0, other, own)], axis=0
        )

    def halves(value):
        half = value.shape[1] // 2
        return value[:, :half], value[:, half:]

    def trade(parts):
        first = jnp.concatenate([halves(part)[0] for part in parts], axis=1)
        second = jnp.concatenate([halves(part)[1] for part in parts], axis=1)
        own = jnp.where(xh == 0, first, second)
        other = team_swap(jnp.where(xh == 0, second, first), 1, 0, 0)
        return both_rows(own, other)

    attend_rows = trade([joint_weight, mixing_weight.T])
    left, right = grid_gather(attend_rows)
    feed_rows = trade([gate_weight, up_weight, down_weight.T])
    feed_weights = lax.all_gather(feed_rows, GRID, axis=0, tiled=True)
    gain_one, gain_two = gather_gains(jnp.concatenate([attend_gain, feed_gain])[None], xh)
    gain_one, gain_two = gain_one.astype(f32), gain_two.astype(f32)

    own_tokens, cotangent_own, feed_own = reorder(tokens[:, 0], cotangent[:, 0])
    all_tokens = team_gather(own_tokens)
    trees = jnp.concatenate([lengths, parents], axis=0)
    trees = jnp.stack([trees, team_swap(trees, 1, 0, 0)])
    chunk = jnp.arange(4, dtype=jnp.int32)
    place = ((xl ^ (chunk // 2)) * 2 + (core ^ (chunk % 2))) * 128
    place = (place[:, None] + jnp.arange(128, dtype=jnp.int32)[None]).reshape(512)
    position, mask = tree_tables(trees[:, 0], trees[:, 1], place)
    cosine, sine = rotary_tables(position)

    wide = all_tokens.astype(f32)
    wide_scale = lax.rsqrt(jnp.mean(wide * wide, axis=1, keepdims=True) + EPSILON)
    normed_one = (wide * wide_scale * gain_one).astype(bf16)

    attend_weights, qkv, mixed, keep, send = attend(
        me, normed_one, left, right, cosine, sine, mask
    )
    incoming = own_tokens.astype(f32)
    middle = incoming + team_scatter(keep, send)
    scale_two = lax.rsqrt(jnp.mean(middle * middle, axis=1, keepdims=True) + EPSILON)
    normed_two = team_gather((middle * scale_two * gain_two).astype(bf16))

    feed_all = team_gather(feed_own)
    slopes = hidden_slopes(feed_all, feed_weights)
    slopes = feed_forward(normed_two, feed_weights, slopes)
    feed_grad = feed_grads(normed_two, feed_all, slopes)
    feed_sum = lax.psum_scatter(feed_grad, GRID, scatter_dimension=0, tiled=True)

    middle_slope = cotangent_own + norm_back(
        team_scatter(*normed_slopes(slopes, feed_weights)), middle, scale_two, gain_two
    )
    branch = team_gather(middle_slope.astype(bf16))
    left, right, keep, send = attend_back(
        me, branch, normed_one, attend_weights, qkv, mixed, cosine, sine, mask
    )
    attend_sum = grid_scatter(left, right).astype(bf16)
    scale_one = lax.rsqrt(jnp.mean(incoming * incoming, axis=1, keepdims=True) + EPSILON)
    input_gradient = middle_slope + norm_back(
        team_scatter(keep, send), incoming, scale_one, gain_one
    )
    layer_output = middle + team_scatter(*down(slopes, feed_weights))

    def home(total, widths):
        rows = total.shape[0] // 2
        own = jnp.where(xh == 0, total[:rows], total[rows:])
        other = team_swap(jnp.where(xh == 0, total[rows:], total[:rows]), 1, 0, 0)
        first = jnp.where(xh == 0, own, other).astype(f32)
        second = jnp.where(xh == 0, other, own).astype(f32)
        out, at = [], 0
        for width in widths:
            out.append(
                jnp.concatenate([first[:, at : at + width], second[:, at : at + width]], axis=1)
            )
            at += width
        return out

    gate_grad, up_grad, down_grad = home(feed_sum, (1024, 1024, 1024))
    joint_grad, mixing_grad = home(attend_sum, (512, 256))

    attend_part = jnp.sum(joint_weight.astype(f32) * joint_grad, axis=1)
    feed_part = jnp.sum(
        gate_weight.astype(f32) * gate_grad + up_weight.astype(f32) * up_grad, axis=1
    )
    attend_total, feed_total = lax.psum((attend_part, feed_part), ("xl", "core"))
    return (
        lane_back(layer_output)[:, None],
        lane_back(input_gradient)[:, None],
        attend_total / attend_gain.astype(f32),
        joint_grad,
        mixing_grad.T,
        feed_total / feed_gain.astype(f32),
        gate_grad,
        up_grad,
        down_grad.T,
    )


def solution(mesh):
    fine = Mesh(mesh.devices.reshape(4, 2, 4, 2, 2), ("z", "xh", "y", "xl", "core"))
    fsdp = ("z", "xh", "y")
    tensor = ("xl", "core")
    in_specs = (
        P(tensor, fsdp, None),
        P(fsdp),
        P(fsdp, tensor),
        P(tensor, fsdp),
        P(fsdp),
        P(fsdp, tensor),
        P(fsdp, tensor),
        P(tensor, fsdp),
        P(fsdp, None),
        P(fsdp, None),
        P(tensor, fsdp, None),
    )
    out_specs = (
        P(tensor, fsdp, None),
        P(tensor, fsdp, None),
        P(fsdp),
        P(fsdp, tensor),
        P(tensor, fsdp),
        P(fsdp),
        P(fsdp, tensor),
        P(fsdp, tensor),
        P(tensor, fsdp),
    )
    return jax.shard_map(shards, mesh=fine, in_specs=in_specs, out_specs=out_specs, check_vma=False)
```

```python
import math

import jax
import jax.numpy as jnp
from jax import lax
from jax.experimental import pallas as pl
from jax.experimental.pallas import tpu as pltpu
from jax.sharding import Mesh
from jax.sharding import PartitionSpec as P

HEADS = 16
KVH = 8
HD = 128
EPSILON = 1e-06
ROPE_BASE = 1000000.0
NEGATIVE = -1e30
MIB = 1024 * 1024
COST = pl.CostEstimate(flops=1 << 20, bytes_accessed=1 << 17, transcendentals=0)

TEAM = ("xh", "xl", "core")
GRID = ("z", "y")

bf16 = jnp.bfloat16
f32 = jnp.float32


def team_swap(value, a, b, c):
    flip = a * 4 + b * 2 + c
    with jax.named_scope(f"team_{a}{b}{c}"):
        return lax.ppermute(value, TEAM, [(i, i ^ flip) for i in range(8)])


def axis_swap(value, axis, flip):
    with jax.named_scope(f"grid_{axis}{flip}"):
        return lax.ppermute(value, axis, [(i, i ^ flip) for i in range(4)])


def after(value, *others):
    return lax.optimization_barrier((value, others))[0]


@jax.named_scope("gather_start")
def gather_start(own):
    return team_swap(own, 0, 1, 0), team_swap(own, 1, 1, 0)


@jax.named_scope("gather_next")
def gather_next(own, started):
    near, next_ = started
    half = near.shape[0] // 2
    pair = jnp.concatenate([own, near], axis=0)
    return (
        pair,
        team_swap(near[:half], 1, 1, 0),
        team_swap(next_[half:], 0, 1, 0),
        team_swap(pair, 0, 0, 1),
    )


def gather_first(later):
    return jnp.concatenate([later[0], later[3]], axis=0)


@jax.named_scope("gather_end")
def gather_pairs(started, later):
    pair = jnp.concatenate([later[1], later[2], started[1]], axis=0)
    return pair, team_swap(pair, 0, 0, 1)


def gather_second(started, later):
    return jnp.concatenate(gather_pairs(started, later), axis=0)


@jax.named_scope("scatter_start")
def scatter_start(part):
    keep, send = part
    return keep, team_swap(send, 0, 0, 1)


def scatter_low(started):
    keep, got = started
    return (keep.astype(f32) + got.astype(f32)).astype(bf16)


@jax.named_scope("scatter_next")
def scatter_next(low, tree):
    if tree == 0:
        return (team_swap(low[128:], 0, 1, 0),)
    return team_swap(low[128:], 1, 1, 0), team_swap(low[:128], 1, 0, 0)


def scatter_end(started, later):
    keep, got = started
    here = keep[:128].astype(f32) + got[:128].astype(f32)
    return sum((item.astype(f32) for item in later), here)


STREAMS = (("z", 1, 3), ("z", 3, 1), ("y", 1, 3), ("y", 3, 1))


def stream_order(stream):
    _, first, second = STREAMS[stream]
    return (0, second, first, 2)


def stream_swap(values, step):
    out = []
    for (axis, first, second), value in zip(STREAMS, values):
        if step >= 2:
            axis = "y" if axis == "z" else "z"
        out.append(axis_swap(value, axis, second if step % 2 else first))
    return out


def add_kernel(*refs):
    count = len(refs) // 4
    for i in range(count):
        total = refs[i][...].astype(f32) + refs[count + i][...].astype(f32)
        low = total.astype(bf16)
        half = low.shape[0] // 2
        refs[2 * count + i][...] = low[:half]
        refs[3 * count + i][...] = low[half:]


def add_streams(stay, came):
    half = jax.ShapeDtypeStruct((stay[0].shape[0] // 2,) + stay[0].shape[1:], bf16)
    out = pl.pallas_call(
        add_kernel,
        out_shape=(half,) * 8,
        compiler_params=pltpu.CompilerParams(vmem_limit_bytes=60 * MIB),
    )(*stay, *came)
    return out[:4], out[4:]


def grid_scatter(stay, go, early, middle, late):
    for step in range(3):
        came = stream_swap(go, step)
        if step == 0:
            came, early = after((came, early))
        if step == 1:
            stay = [value.reshape(4, 32, 768) for value in stay]
            came = [value.reshape(4, 32, 768) for value in came]
            came, middle = after((came, middle))
        stay, go = add_streams(stay, came)
    go, late = after((go, late))
    came = stream_swap(go, 3)
    total = jnp.concatenate(
        [(a[0].astype(f32) + b[0].astype(f32)).astype(bf16) for a, b in zip(stay, came)], axis=0
    )
    return total, early, middle, late


def lane_order(value):
    parts = []
    for z in range(4):
        for y in range(4):
            for xh in range(2):
                start = z * 512 + xh * 256 + y * 64
                parts.append(value[:, start : start + 64])
    return jnp.concatenate(parts, axis=1)


def lane_back(value):
    parts = []
    for z in range(4):
        for xh in range(2):
            for y in range(4):
                start = z * 512 + y * 128 + xh * 64
                parts.append(value[:, start : start + 64])
    return jnp.concatenate(parts, axis=1)


SCALARS = pl.BlockSpec(memory_space=pltpu.SMEM)
VECTORS = pl.BlockSpec(memory_space=pltpu.VMEM)


def put_halves(value, at, stay, own_ref, send_ref):
    half = value.shape[1] // 2
    first, second = value[:, :half], value[:, half:]
    own_ref[:, at : at + half] = jnp.where(stay, first, second)
    send_ref[:, at : at + half] = jnp.where(stay, second, first)


def prepare_kernel(
    me_ref, tokens_ref, slope_ref, joint_ref, mixing_ref, gain_ref,
    rows_out, slope_out, own_ref, send_ref,
):
    rows_out[0:128, :] = lane_order(tokens_ref[...].astype(f32)).astype(bf16)
    slope = lane_order(slope_ref[...])
    slope_out[...] = slope
    rows_out[128:256, :] = slope.astype(bf16)
    stay = me_ref[3] == 0
    put_halves(joint_ref[...], 0, stay, own_ref, send_ref)
    put_halves(mixing_ref[...], 512, stay, own_ref, send_ref)
    gains = jnp.broadcast_to(gain_ref[...].astype(f32), (128, 128)).T
    lane = lax.broadcasted_iota(jnp.int32, (64, 128), 1)
    gains = jnp.where(lane == 0, gains[0:64], gains[64:128]).astype(bf16)
    own_ref[:, 768:896] = gains
    send_ref[:, 768:896] = gains


def prepare(me, tokens, slope, joint, mixing, gains):
    return pl.pallas_call(
        prepare_kernel,
        in_specs=[SCALARS] + [VECTORS] * 5,
        out_specs=[VECTORS] * 4,
        out_shape=(
            jax.ShapeDtypeStruct((256, 2048), bf16),
            jax.ShapeDtypeStruct(slope.shape, f32),
            jax.ShapeDtypeStruct((64, 896), bf16),
            jax.ShapeDtypeStruct((64, 896), bf16),
        ),
        compiler_params=pltpu.CompilerParams(vmem_limit_bytes=60 * MIB),
    )(me, tokens, slope, joint, mixing, gains)


def prepare_feed_kernel(me_ref, gate_ref, up_ref, down_ref, own_ref, send_ref):
    stay = me_ref[3] == 0
    put_halves(gate_ref[...], 0, stay, own_ref, send_ref)
    put_halves(up_ref[...], 1024, stay, own_ref, send_ref)
    put_halves(down_ref[...], 2048, stay, own_ref, send_ref)


def prepare_feed(me, gate, up, down_weight):
    return pl.pallas_call(
        prepare_feed_kernel,
        in_specs=[SCALARS] + [VECTORS] * 3,
        out_specs=[VECTORS] * 2,
        out_shape=(
            jax.ShapeDtypeStruct((64, 3072), bf16),
            jax.ShapeDtypeStruct((64, 3072), bf16),
        ),
        compiler_params=pltpu.CompilerParams(vmem_limit_bytes=60 * MIB),
    )(me, gate, up, down_weight)


def rows_kernel(me_ref, own_ref, other_ref, out_ref):
    stay = me_ref[3] == 0
    own, other = own_ref[...], other_ref[...]
    out_ref[0:64, :] = jnp.where(stay, own, other)
    out_ref[64:128, :] = jnp.where(stay, other, own)


def place_rows(me, own, other):
    return pl.pallas_call(
        rows_kernel,
        in_specs=[SCALARS] + [VECTORS] * 2,
        out_specs=VECTORS,
        out_shape=jax.ShapeDtypeStruct((128, own.shape[1]), bf16),
        compiler_params=pltpu.CompilerParams(vmem_limit_bytes=32 * MIB),
    )(me, own, other)


def tree_tables(lengths, parents, place):
    nseg = lengths.shape[1]
    batch = lengths.shape[0]
    ends = jnp.cumsum(lengths, axis=1)
    starts = ends - lengths
    segment = jnp.sum((place[None, :, None] >= ends[:, None, : nseg - 1]).astype(jnp.int32), axis=2)
    order = jnp.arange(nseg, dtype=jnp.int32)
    rows = [(order == 0).astype(f32)[None, :] * jnp.ones((batch, 1), f32)]
    depth = [jnp.zeros((batch,), jnp.int32)]
    for later in range(1, nseg):
        above = jnp.zeros_like(rows[0])
        reach = jnp.zeros_like(depth[0])
        for earlier in range(later):
            hit = parents[:, later] == earlier
            above = above + hit.astype(f32)[:, None] * rows[earlier]
            reach = reach + jnp.where(hit, depth[earlier] + lengths[:, earlier], 0)
        rows.append(above + (order == later).astype(f32)[None, :])
        depth.append(reach)
    ancestry = jnp.stack(rows, axis=1)
    begin = jnp.stack(depth, axis=1)
    pick = (segment[:, :, None] == order[None, None, :]).astype(f32)
    shift = (begin - starts).astype(f32)
    position = place[None, :].astype(f32) + jnp.sum(pick * shift[:, None, :], axis=2)
    linked = jnp.einsum("bis,bst,bjt->bij", pick, ancestry, pick)
    causal = place[None, :] <= place[:, None]
    return position, ((linked > 0.5) & causal[None]).astype(bf16)


def rotary_tables(position):
    half = HD // 2
    rates = jnp.exp(jnp.arange(half, dtype=f32) * (-2.0 * math.log(ROPE_BASE) / HD))
    angle = position[..., None] * rates
    cosine, sine = jnp.cos(angle), jnp.sin(angle)
    return jnp.concatenate([cosine, cosine], axis=-1), jnp.concatenate([-sine, sine], axis=-1)


def dot(left, right, contract):
    return lax.dot_general(
        left, right, (((contract[0],), (contract[1],)), ((), ())), preferred_element_type=f32
    )


def turn(value, cosine, sine):
    return value * cosine + pltpu.roll(value, HD // 2, 1) * sine


def attend_kernel(
    me_ref, x0_ref, x1_ref, x2_ref, x3_ref, w_ref, gain_ref, cos_ref, sin_ref, mask_ref,
    gains_out, n_ref, qkv_ref, mixed_ref, keep_ref, send_ref,
):
    gains = gain_ref[...].astype(f32).T[0:8, :]
    gains_out[...] = gains
    for k, x_ref in enumerate((x0_ref, x1_ref, x2_ref, x3_ref)):
        wide = x_ref[...].astype(f32)
        scale = lax.rsqrt(jnp.mean(wide * wide, axis=1, keepdims=True) + EPSILON)
        n_ref[k * 128 : k * 128 + 128, :] = (wide * scale * gains[0:1, :]).astype(bf16)
    joint = dot(n_ref[...], w_ref[:, 0:512], (1, 0))
    cosine, sine = cos_ref[0], sin_ref[0]
    keys = turn(joint[:, 256:384], cosine, sine).astype(bf16)
    values = joint[:, 384:512].astype(bf16)
    qkv_ref[:, 256:384] = keys
    qkv_ref[:, 384:512] = values
    allowed = mask_ref[0].astype(f32) > 0.5
    for head in range(2):
        at = slice(head * HD, head * HD + HD)
        queries = turn(joint[:, at], cosine, sine).astype(bf16)
        qkv_ref[:, at] = queries
        scores = dot(queries, keys, (1, 1)) * (1.0 / math.sqrt(HD))
        scores = jnp.where(allowed, scores, NEGATIVE)
        powers = jnp.exp(scores - jnp.max(scores, axis=1, keepdims=True))
        chance = (powers / jnp.sum(powers, axis=1, keepdims=True)).astype(bf16)
        mixed_ref[:, at] = dot(chance, values, (1, 0)).astype(bf16)
    part = dot(mixed_ref[...], w_ref[:, 512:768], (1, 1)).astype(bf16)
    keep_ref[...] = part[0:256]
    send_ref[...] = part[256:512]


def rows_of(mine, other):
    return mine, mine, other, other


def whole(shape):
    return pl.BlockSpec(shape, lambda i, me: (0,) * len(shape))


ATTEND_COLUMNS = pl.BlockSpec((2048, 768), lambda i, me: (0, 0))
GAIN_COLUMNS = pl.BlockSpec((2048, 128), lambda i, me: (0, 6))


def attend(me, tokens, weights, cosine, sine, mask, tree):
    table = lambda width: pl.BlockSpec((1, 512, width), lambda i, me: (tree, 0, 0))
    shapes = [
        ((8, 2048), f32), ((512, 2048), bf16), ((512, 512), bf16), ((512, 256), bf16),
        ((256, 2048), bf16), ((256, 2048), bf16),
    ]
    return pl.pallas_call(
        attend_kernel,
        grid_spec=pltpu.PrefetchScalarGridSpec(
            num_scalar_prefetch=1,
            grid=(1,),
            in_specs=[pl.BlockSpec((128, 2048), lambda i, me, k=k: (k, 0)) for k in (0, 2)] * 2
            + [ATTEND_COLUMNS, GAIN_COLUMNS, table(HD), table(HD), table(512)],
            out_specs=[whole(shape) for shape, _ in shapes],
        ),
        out_shape=[jax.ShapeDtypeStruct(shape, kind) for shape, kind in shapes],
        compiler_params=pltpu.CompilerParams(vmem_limit_bytes=56 * MIB),
        cost_estimate=COST,
    )(me, *rows_of(*tokens), weights, weights, cosine, sine, mask)


def attend_back_tree(branch_ref, w_ref, qkv_ref, cos_ref, sin_ref, mask_ref, keep_ref, send_ref,
                     js_ref):
    factor = 1.0 / math.sqrt(HD)
    mixed_slope = dot(branch_ref[...], w_ref[:, 512:768], (1, 0)).astype(bf16)
    cosine, sine = cos_ref[0], -sin_ref[0]
    allowed = mask_ref[0].astype(f32) > 0.5
    keys = qkv_ref[:, 256:384]
    values = qkv_ref[:, 384:512]
    key_slope = jnp.zeros((512, HD), f32)
    value_slope = jnp.zeros((512, HD), f32)
    for head in range(2):
        at = slice(head * HD, head * HD + HD)
        queries = qkv_ref[:, at]
        scores = jnp.where(allowed, dot(queries, keys, (1, 1)) * factor, NEGATIVE)
        powers = jnp.exp(scores - jnp.max(scores, axis=1, keepdims=True))
        chance = powers / jnp.sum(powers, axis=1, keepdims=True)
        slope = mixed_slope[:, at]
        value_slope += dot(chance.astype(bf16), slope, (0, 0))
        chance_slope = dot(slope, values, (1, 1))
        balance = jnp.sum(chance * chance_slope, axis=1, keepdims=True)
        score_slope = (chance * (chance_slope - balance)).astype(bf16)
        query_slope = dot(score_slope, keys, (1, 0)) * factor
        js_ref[:, at] = turn(query_slope, cosine, sine).astype(bf16)
        key_slope += dot(score_slope, queries, (0, 0)) * factor
    js_ref[:, 256:384] = turn(key_slope, cosine, sine).astype(bf16)
    js_ref[:, 384:512] = value_slope.astype(bf16)
    part = dot(js_ref[...], w_ref[:, 0:512], (1, 1)).astype(bf16)
    keep_ref[...] = part[0:256]
    send_ref[...] = part[256:512]


def attend_back_first_kernel(
    me_ref, branch_ref, w_ref, qkv_ref, cos_ref, sin_ref, mask_ref, keep_ref, send_ref, js_ref
):
    attend_back_tree(
        branch_ref, w_ref, qkv_ref, cos_ref, sin_ref, mask_ref, keep_ref, send_ref, js_ref
    )


def attend_back_second_kernel(
    me_ref, branch_ref, w_ref, qkv_ref, cos_ref, sin_ref, mask_ref,
    other_branch, other_js, n0_ref, n1_ref, mixed0_ref, mixed1_ref, *refs,
):
    keep_ref, send_ref = refs[0:2]
    stay_refs, go_refs = refs[2:6], refs[6:10]
    js_ref, joint_acc, mixing_acc = refs[10:13]
    z, y = me_ref[0], me_ref[1]
    attend_back_tree(
        branch_ref, w_ref, qkv_ref, cos_ref, sin_ref, mask_ref, keep_ref, send_ref, js_ref
    )
    joint_acc[...] = dot(n0_ref[...], other_js[...], (0, 0)) + dot(n1_ref[...], js_ref[...], (0, 0))
    mixing_acc[...] = dot(other_branch[...], mixed0_ref[...], (0, 0)) + dot(
        branch_ref[...], mixed1_ref[...], (0, 0)
    )
    for stream in range(4):
        order = stream_order(stream)
        for i in range(4):
            for j in range(4):
                dz, dy = (order[i], order[j]) if stream < 2 else (order[j], order[i])
                first = ((z ^ dz) * 4 + (y ^ dy)) * 128 + stream * 32
                rows = pl.ds(pl.multiple_of(first, 32), 32)
                out = stay_refs[stream] if i < 2 else go_refs[stream]
                out[i % 2, j, :, 0:512] = joint_acc[rows, :].astype(bf16)
                out[i % 2, j, :, 512:768] = mixing_acc[rows, :].astype(bf16)


def attend_back(me, branch, weights, qkv, cosine, sine, mask, tree, others=None):
    table = lambda width: pl.BlockSpec((1, 512, width), lambda i, me: (tree, 0, 0))
    part = ((256, 2048), bf16)
    shapes = [part, part]
    scratch = []
    if others is None:
        shapes.append(((512, 512), bf16))
    else:
        shapes += [((2, 4, 32, 768), bf16)] * 8
        scratch = [
            pltpu.VMEM((512, 512), bf16), pltpu.VMEM((2048, 512), f32), pltpu.VMEM((2048, 256), f32)
        ]
    extra = () if others is None else others
    return pl.pallas_call(
        attend_back_first_kernel if others is None else attend_back_second_kernel,
        grid_spec=pltpu.PrefetchScalarGridSpec(
            num_scalar_prefetch=1,
            grid=(1,),
            in_specs=[whole((512, 2048)), ATTEND_COLUMNS, whole((512, 512))]
            + [table(HD), table(HD), table(512)]
            + [whole(item.shape) for item in extra],
            out_specs=[whole(shape) for shape, _ in shapes],
            scratch_shapes=scratch,
        ),
        out_shape=[jax.ShapeDtypeStruct(shape, kind) for shape, kind in shapes],
        compiler_params=pltpu.CompilerParams(vmem_limit_bytes=56 * MIB),
        cost_estimate=COST,
    )(me, branch, weights, qkv, cosine, sine, mask, *extra)


SLOPE_CHUNKS = [pl.BlockSpec((128, 2048), lambda j, k=k: (k, 0)) for k in (1, 3)] * 2


def hidden_slope_kernel(*refs):
    x_refs, w_ref, o_ref, whole_ref = refs[:8], refs[8], refs[9], refs[10]

    @pl.when(pl.program_id(0) == 0)
    def _():
        for k in range(8):
            whole_ref[k * 128 : k * 128 + 128, :] = x_refs[k][...]

    o_ref[...] = dot(whole_ref[...], w_ref[...], (1, 0))


def hidden_slopes(feed0, feed1, weights):
    return pl.pallas_call(
        hidden_slope_kernel,
        grid=(4,),
        in_specs=SLOPE_CHUNKS * 2 + [pl.BlockSpec((2048, 256), lambda j: (0, j + 8))],
        out_specs=pl.BlockSpec((1024, 256), lambda j: (0, j)),
        out_shape=jax.ShapeDtypeStruct((1024, 1024), f32),
        scratch_shapes=[pltpu.VMEM((1024, 2048), bf16)],
        compiler_params=pltpu.CompilerParams(vmem_limit_bytes=48 * MIB),
        cost_estimate=COST,
    )(*rows_of(*feed0), *rows_of(*feed1), weights)


def feed_kernel(n0_ref, n1_ref, gate_ref, up_ref, slope_ref, out0_ref, out1_ref):
    for tree, (n_ref, out_ref) in enumerate(((n0_ref, out0_ref), (n1_ref, out1_ref))):
        gate = dot(n_ref[...], gate_ref[...], (1, 0))
        upper = dot(n_ref[...], up_ref[...], (1, 0))
        slope = slope_ref[tree * 512 : tree * 512 + 512, :]
        sigma = jax.nn.sigmoid(gate)
        active = gate * sigma
        out_ref[0] = (slope * upper * sigma * (1.0 + gate * (1.0 - sigma))).astype(bf16)
        out_ref[1] = (slope * active).astype(bf16)
        out_ref[2] = (active * upper).astype(bf16)


def feed_forward(normed, weights, slopes):
    return pl.pallas_call(
        feed_kernel,
        grid=(4,),
        in_specs=[
            pl.BlockSpec((512, 2048), lambda j: (0, 0)),
            pl.BlockSpec((512, 2048), lambda j: (0, 0)),
            pl.BlockSpec((2048, 256), lambda j: (0, j)),
            pl.BlockSpec((2048, 256), lambda j: (0, j + 4)),
            pl.BlockSpec((1024, 256), lambda j: (0, j)),
        ],
        out_specs=[pl.BlockSpec((3, 512, 256), lambda j: (0, 0, j))] * 2,
        out_shape=(jax.ShapeDtypeStruct((3, 512, 1024), bf16),) * 2,
        compiler_params=pltpu.CompilerParams(vmem_limit_bytes=48 * MIB),
        cost_estimate=COST,
    )(*normed, weights, weights, slopes)


def feed_grad_kernel(*refs):
    n_refs, f_refs = refs[0:2], refs[2:10]
    s0_ref, s1_ref, out_ref, turned = refs[10:14]
    step = pl.program_id(0)

    @pl.when(step == 0)
    def _():
        for k in range(2):
            turned[:, k * 512 : k * 512 + 512] = n_refs[k][...].T

    @pl.when(step == 8)
    def _():
        for k in range(8):
            turned[:, k * 128 : k * 128 + 128] = f_refs[k][...].T

    slopes = jnp.concatenate([s0_ref[0], s1_ref[0]], axis=0)
    out_ref[...] = dot(turned[...], slopes, (1, 0)).astype(bf16)


def feed_grads(normed, feed0, feed1, slopes):
    return pl.pallas_call(
        feed_grad_kernel,
        grid=(12,),
        in_specs=[pl.BlockSpec((512, 2048), lambda j: (0, 0))] * 2
        + SLOPE_CHUNKS * 2
        + [pl.BlockSpec((1, 512, 256), lambda j: (j // 4, 0, j % 4))] * 2,
        out_specs=pl.BlockSpec((2048, 256), lambda j: (0, j)),
        out_shape=jax.ShapeDtypeStruct((2048, 3072), bf16),
        scratch_shapes=[pltpu.VMEM((2048, 1024), bf16)],
        compiler_params=pltpu.CompilerParams(vmem_limit_bytes=48 * MIB),
        cost_estimate=COST,
    )(*normed, *rows_of(*feed0), *rows_of(*feed1), *slopes)


def split_rows(part, keep_ref, send_ref):
    keep_ref[...] = part[0:256]
    send_ref[...] = part[256:512]


def normed_slope_kernel(g_ref, u_ref, wg_ref, wu_ref, keep_ref, send_ref):
    part = dot(g_ref[0], wg_ref[...], (1, 1)) + dot(u_ref[0], wu_ref[...], (1, 1))
    split_rows(part.astype(bf16), keep_ref, send_ref)


def normed_slopes(slopes, weights):
    half = jax.ShapeDtypeStruct((256, 2048), bf16)
    return pl.pallas_call(
        normed_slope_kernel,
        grid=(4,),
        in_specs=[
            pl.BlockSpec((1, 512, 1024), lambda j: (0, 0, 0)),
            pl.BlockSpec((1, 512, 1024), lambda j: (1, 0, 0)),
            pl.BlockSpec((512, 1024), lambda j: (j, 0)),
            pl.BlockSpec((512, 1024), lambda j: (j, 1)),
        ],
        out_specs=[pl.BlockSpec((256, 512), lambda j: (0, j))] * 2,
        out_shape=(half, half),
        compiler_params=pltpu.CompilerParams(vmem_limit_bytes=48 * MIB),
        cost_estimate=COST,
    )(slopes, slopes, weights, weights)


def down_kernel(h_ref, w_ref, keep_ref, send_ref):
    split_rows(dot(h_ref[0], w_ref[...], (1, 1)).astype(bf16), keep_ref, send_ref)


def down(slopes, weights):
    half = jax.ShapeDtypeStruct((256, 2048), bf16)
    return pl.pallas_call(
        down_kernel,
        grid=(4,),
        in_specs=[
            pl.BlockSpec((1, 512, 1024), lambda j: (2, 0, 0)),
            pl.BlockSpec((512, 1024), lambda j: (j, 2)),
        ],
        out_specs=[pl.BlockSpec((256, 512), lambda j: (0, j))] * 2,
        out_shape=(half, half),
        compiler_params=pltpu.CompilerParams(vmem_limit_bytes=48 * MIB),
        cost_estimate=COST,
    )(slopes, weights)


def norm_back(slope, incoming, scale, gain):
    weighted = slope * gain
    cubed = scale * scale * scale
    return scale * weighted - incoming * cubed * jnp.mean(weighted * incoming, axis=1, keepdims=True)


def shards(
    tokens, attend_gain, joint_weight, mixing_weight, feed_gain, gate_weight, up_weight,
    down_weight, lengths, parents, cotangent,
):
    z, y = lax.axis_index("z"), lax.axis_index("y")
    xh, xl, core = lax.axis_index("xh"), lax.axis_index("xl"), lax.axis_index("core")
    me = jnp.stack([z, y, xh * 4 + xl * 2 + core, xh]).astype(jnp.int32)

    def home_start(total):
        rows = total.shape[0] // 2
        own = jnp.where(xh == 0, total[:rows], total[rows:])
        return own, team_swap(jnp.where(xh == 0, total[rows:], total[:rows]), 1, 0, 0)

    def home_end(own, other, widths):
        first = jnp.where(xh == 0, own, other).astype(f32)
        second = jnp.where(xh == 0, other, own).astype(f32)
        out, at = [], 0
        for width in widths:
            out.append(
                jnp.concatenate([first[:, at : at + width], second[:, at : at + width]], axis=1)
            )
            at += width
        return out

    gains = jnp.concatenate([attend_gain, feed_gain])[None]
    own_rows, cotangent_own, own, send = prepare(
        me, tokens[:, 0], cotangent[:, 0], joint_weight, mixing_weight.T, gains
    )
    other = team_swap(send, 1, 0, 0)
    trees = jnp.concatenate([lengths, parents], axis=0)
    trees_other = team_swap(trees, 1, 0, 0)
    feed_stay, feed_send = prepare_feed(me, gate_weight, up_weight, down_weight.T)
    attend_rows = place_rows(me, own, other)
    weights = lax.all_gather(attend_rows, GRID, axis=0, tiled=True)

    rows_started = gather_start(after(own_rows, attend_rows))
    feed_other = team_swap(after(feed_send, attend_rows), 1, 0, 0)
    feed_rows = place_rows(me, feed_stay, feed_other)
    feed_weights = lax.all_gather(feed_rows, GRID, axis=0, tiled=True)
    trees = jnp.stack([trees, trees_other])
    chunk = jnp.arange(4, dtype=jnp.int32)
    place = ((xl ^ (chunk % 2)) * 2 + (core ^ (chunk // 2))) * 128
    place = (place[:, None] + jnp.arange(128, dtype=jnp.int32)[None]).reshape(512)
    position, mask = tree_tables(trees[:, 0], trees[:, 1], place)
    cosine, sine = rotary_tables(position)
    rows_started, feed_rows, mask, cosine, sine = after(
        (rows_started, feed_rows, mask, cosine, sine)
    )
    rows_later = gather_next(own_rows, rows_started)
    rows0 = (rows_later[0], rows_later[3])
    rows1 = gather_pairs(rows_started, rows_later)
    rows0, rows1, weights = after((rows0, rows1, weights))

    gains, normed1, qkv1, mixed1, *part1 = attend(me, rows1, weights, cosine, sine, mask, 1)
    mixing1 = scatter_start(part1)
    low1 = scatter_low(mixing1)
    mixing1_later = scatter_next(low1, 1)
    _, normed0, qkv0, mixed0, *part0 = attend(
        me, after(rows0, low1), weights, cosine, sine, mask, 0
    )
    mixing0 = scatter_start(part0)
    low0 = scatter_low(mixing0)
    mixing0_later = scatter_next(low0, 0)
    gain_one, gain_two = gains[0:1], gains[1:2]
    incoming = own_rows[:128].astype(f32)
    middle = incoming + scatter_end(mixing0, mixing0_later + mixing1_later)
    scale_two = lax.rsqrt(jnp.mean(middle * middle, axis=1, keepdims=True) + EPSILON)
    own_normed = (middle * scale_two * gain_two).astype(bf16)
    normed_started = gather_start(own_normed)
    normed_later = gather_next(own_normed, normed_started)
    two0 = gather_first(normed_later)
    two1 = gather_second(normed_started, normed_later)
    hidden_slope = hidden_slopes(rows0, rows1, feed_weights)
    slopes = slopes0, slopes1 = feed_forward((two0, two1), feed_weights, hidden_slope)
    slope1 = scatter_start(normed_slopes(slopes1, feed_weights))
    low1 = scatter_low(slope1)
    slope1_later = scatter_next(low1, 1)
    slope0 = scatter_start(normed_slopes(after(slopes0, low1), feed_weights))
    low0 = scatter_low(slope0)
    slope0_later = scatter_next(low0, 0)
    feed_grad = feed_grads((two0, two1), rows0, rows1, after(slopes, low0))
    slope0_later, slope1_later, feed_grad = after((slope0_later, slope1_later, feed_grad))
    feed_sum = lax.psum_scatter(feed_grad, GRID, scatter_dimension=0, tiled=True)

    middle_slope = cotangent_own + norm_back(
        scatter_end(slope0, slope0_later + slope1_later), middle, scale_two, gain_two
    )
    low = middle_slope.astype(bf16)
    branch_started = gather_start(low)
    down0, down1 = down(after(slopes0, low), feed_weights), down(after(slopes1, low), feed_weights)
    branch_started, down0, down1 = after((branch_started, down0, down1))
    branch_later = gather_next(low, branch_started)
    down0, down1 = scatter_start(down0), scatter_start(down1)
    branch0 = gather_first(branch_later)
    keep0, send0, js0 = attend_back(
        me, branch0, weights, qkv0, cosine, sine, mask, 0
    )
    input0 = scatter_start((keep0, send0))
    branch1 = gather_second(branch_started, branch_later)

    down0_low, down1_low = scatter_low(down0), scatter_low(down1)
    down0_later = scatter_next(down0_low, 0)
    down1_later = scatter_next(down1_low, 1)
    input0_low = scatter_low(input0)
    input0_later = scatter_next(input0_low, 0)
    keep1, send1, *streams = attend_back(
        me, after(branch1, js0, down0_low, down1_low, input0_low), weights, qkv1, cosine, sine,
        mask, 1, (branch0, js0, normed0, normed1, mixed0, mixed1),
    )
    input1 = scatter_start((keep1, send1))
    input1_later = scatter_next(scatter_low(input1), 1)
    feed_own, feed_other = home_start(feed_sum)
    attend_sum, (down0_later, down1_later, input0_later), input1_later, feed_other = grid_scatter(
        streams[:4], streams[4:], (down0_later, down1_later, input0_later), input1_later,
        feed_other,
    )
    layer_output = middle + scatter_end(down0, down0_later + down1_later)
    attend_own, attend_other = home_start(attend_sum)
    scale_one = lax.rsqrt(jnp.mean(incoming * incoming, axis=1, keepdims=True) + EPSILON)
    input_gradient = middle_slope + norm_back(
        scatter_end(input0, input0_later + input1_later), incoming, scale_one, gain_one
    )
    gate_grad, up_grad, down_grad = home_end(feed_own, feed_other, (1024, 1024, 1024))
    joint_grad, mixing_grad = home_end(attend_own, attend_other, (512, 256))

    attend_part = jnp.sum(joint_weight.astype(f32) * joint_grad, axis=1)
    feed_part = jnp.sum(
        gate_weight.astype(f32) * gate_grad + up_weight.astype(f32) * up_grad, axis=1
    )
    attend_total, feed_total = lax.psum((attend_part, feed_part), ("xl", "core"))
    return (
        lane_back(layer_output)[:, None],
        lane_back(input_gradient)[:, None],
        attend_total / attend_gain.astype(f32),
        joint_grad,
        mixing_grad.T,
        feed_total / feed_gain.astype(f32),
        gate_grad,
        up_grad,
        down_grad.T,
    )


def solution(mesh):
    fine = Mesh(mesh.devices.reshape(4, 2, 4, 2, 2), ("z", "xh", "y", "xl", "core"))
    fsdp = ("z", "xh", "y")
    tensor = ("xl", "core")
    in_specs = (
        P(tensor, fsdp, None),
        P(fsdp),
        P(fsdp, tensor),
        P(tensor, fsdp),
        P(fsdp),
        P(fsdp, tensor),
        P(fsdp, tensor),
        P(tensor, fsdp),
        P(fsdp, None),
        P(fsdp, None),
        P(tensor, fsdp, None),
    )
    out_specs = (
        P(tensor, fsdp, None),
        P(tensor, fsdp, None),
        P(fsdp),
        P(fsdp, tensor),
        P(tensor, fsdp),
        P(fsdp),
        P(fsdp, tensor),
        P(fsdp, tensor),
        P(tensor, fsdp),
    )
    return jax.shard_map(shards, mesh=fine, in_specs=in_specs, out_specs=out_specs, check_vma=False)
```

```python
import math

import jax
import jax.numpy as jnp
from jax import lax
from jax.experimental import pallas as pl
from jax.experimental.pallas import tpu as pltpu
from jax.sharding import Mesh
from jax.sharding import PartitionSpec as P

HEADS = 16
KVH = 8
HD = 128
EPSILON = 1e-06
ROPE_BASE = 1000000.0
NEGATIVE = -1e30
MIB = 1024 * 1024
COST = pl.CostEstimate(flops=1 << 20, bytes_accessed=1 << 17, transcendentals=0)

TEAM = ("xh", "xl", "core")
GRID = ("z", "y")

bf16 = jnp.bfloat16
f32 = jnp.float32


def team_swap(value, a, b, c):
    flip = a * 4 + b * 2 + c
    with jax.named_scope(f"team_{a}{b}{c}"):
        return lax.ppermute(value, TEAM, [(i, i ^ flip) for i in range(8)])


def axis_swap(value, axis, flip):
    with jax.named_scope(f"grid_{axis}{flip}"):
        return lax.ppermute(value, axis, [(i, i ^ flip) for i in range(4)])


def after(value, *others):
    return lax.optimization_barrier((value, others))[0]


@jax.named_scope("gather_start")
def gather_start(own):
    return team_swap(own, 0, 1, 0), team_swap(own, 1, 1, 0)


@jax.named_scope("gather_next")
def gather_next(own, started):
    near, next_ = started
    half = near.shape[0] // 2
    pair = jnp.concatenate([own, near], axis=0)
    return (
        pair,
        team_swap(near[:half], 1, 1, 0),
        team_swap(next_[half:], 0, 1, 0),
        team_swap(pair, 0, 0, 1),
    )


def gather_first(later):
    return later[0], later[3]


@jax.named_scope("gather_end")
def gather_second(started, later):
    pair = jnp.concatenate([later[1], later[2], started[1]], axis=0)
    return pair, team_swap(pair, 0, 0, 1)


@jax.named_scope("scatter_start")
def scatter_start(part):
    keep, send = part
    return keep, team_swap(send, 0, 0, 1)


def scatter_sums(started, tree):
    keep, got = started
    low = keep[:128].astype(f32) + got[:128].astype(f32)
    high = (keep[128:].astype(f32) + got[128:].astype(f32)).astype(bf16)
    return (low.astype(bf16) if tree else low), high


@jax.named_scope("scatter_next")
def scatter_next(sums, tree):
    low, high = sums
    if tree == 0:
        return low, team_swap(high, 0, 1, 0)
    return team_swap(low, 1, 0, 0), team_swap(high, 1, 1, 0)


def total(terms):
    return sum((item.astype(f32) for item in terms[1:]), terms[0].astype(f32))


STREAMS = (("z", 1, 3), ("y", 1, 3))


def stream_order(stream):
    _, first, second = STREAMS[stream]
    return (0, second, first, 2)


def stream_swap(values, step):
    out = []
    for (axis, first, second), value in zip(STREAMS, values):
        if step >= 2:
            axis = "y" if axis == "z" else "z"
        out.append(axis_swap(value, axis, second if step % 2 else first))
    return out


def add_kernel(*refs):
    count = len(refs) // 4
    for i in range(count):
        total = refs[i][...].astype(f32) + refs[count + i][...].astype(f32)
        low = total.astype(bf16)
        half = low.shape[0] // 2
        refs[2 * count + i][...] = low[:half]
        refs[3 * count + i][...] = low[half:]


def add_streams(stay, came):
    half = jax.ShapeDtypeStruct((stay[0].shape[0] // 2,) + stay[0].shape[1:], bf16)
    out = pl.pallas_call(
        add_kernel,
        out_shape=(half,) * (2 * len(stay)),
        compiler_params=pltpu.CompilerParams(vmem_limit_bytes=24 * MIB),
    )(*stay, *came)
    return out[: len(stay)], out[len(stay) :]


def grid_scatter(stay, go, first, second):
    others = [first, second, ()]
    for step in range(3):
        came, others[step] = after((stream_swap(go, step), others[step]))
        if step == 1:
            stay = [value.reshape(4, 64, 768) for value in stay]
            came = [value.reshape(4, 64, 768) for value in came]
        stay, go = add_streams(stay, came)
    came = stream_swap(go, 3)
    rows = jnp.concatenate(
        [(a[0].astype(f32) + b[0].astype(f32)).astype(bf16) for a, b in zip(stay, came)], axis=0
    )
    return rows, *others[:2]


def lane_order(value):
    parts = []
    for z in range(4):
        for y in range(4):
            for xh in range(2):
                start = z * 512 + xh * 256 + y * 64
                parts.append(value[:, start : start + 64])
    return jnp.concatenate(parts, axis=1)


def lane_back(value):
    parts = []
    for z in range(4):
        for xh in range(2):
            for y in range(4):
                start = z * 512 + y * 128 + xh * 64
                parts.append(value[:, start : start + 64])
    return jnp.concatenate(parts, axis=1)


SCALARS = pl.BlockSpec(memory_space=pltpu.SMEM)
VECTORS = pl.BlockSpec(memory_space=pltpu.VMEM)


def put_halves(value, at, stay, own_ref, send_ref):
    half = value.shape[1] // 2
    first, second = value[:, :half], value[:, half:]
    own_ref[:, at : at + half] = jnp.where(stay, first, second)
    send_ref[:, at : at + half] = jnp.where(stay, second, first)


def prepare_attend_kernel(me_ref, joint_ref, mixing_ref, down_ref, gain_ref, own_ref, send_ref):
    stay = me_ref[3] == 0
    put_halves(joint_ref[...], 0, stay, own_ref, send_ref)
    put_halves(mixing_ref[...], 512, stay, own_ref, send_ref)
    put_halves(down_ref[...], 768, stay, own_ref, send_ref)
    gains = jnp.broadcast_to(gain_ref[...].astype(f32), (128, 128)).T
    lane = lax.broadcasted_iota(jnp.int32, (64, 128), 1)
    gains = jnp.where(lane == 0, gains[0:64], gains[64:128]).astype(bf16)
    own_ref[:, 1792:1920] = gains
    send_ref[:, 1792:1920] = gains


def prepare_feed_kernel(me_ref, gate_ref, up_ref, own_ref, send_ref):
    stay = me_ref[3] == 0
    put_halves(gate_ref[...], 0, stay, own_ref, send_ref)
    put_halves(up_ref[...], 1024, stay, own_ref, send_ref)


def prepare_weights(kernel, me, width, *values):
    return pl.pallas_call(
        kernel,
        in_specs=[SCALARS] + [VECTORS] * len(values),
        out_specs=[VECTORS] * 2,
        out_shape=(jax.ShapeDtypeStruct((64, width), bf16),) * 2,
        compiler_params=pltpu.CompilerParams(vmem_limit_bytes=32 * MIB),
    )(me, *values)


def prepare_rows_kernel(tokens_ref, slope_ref, rows_out, slope_out):
    rows_out[0:128, :] = lane_order(tokens_ref[...].astype(f32)).astype(bf16)
    slope = lane_order(slope_ref[...])
    slope_out[...] = slope
    rows_out[128:256, :] = slope.astype(bf16)


def prepare_rows(tokens, slope):
    return pl.pallas_call(
        prepare_rows_kernel,
        out_shape=(
            jax.ShapeDtypeStruct((256, 2048), bf16),
            jax.ShapeDtypeStruct(slope.shape, f32),
        ),
        compiler_params=pltpu.CompilerParams(vmem_limit_bytes=32 * MIB),
    )(tokens, slope)


def rows_kernel(me_ref, own_ref, other_ref, out_ref):
    stay = me_ref[3] == 0
    own, other = own_ref[...], other_ref[...]
    out_ref[0:64, :] = jnp.where(stay, own, other)
    out_ref[64:128, :] = jnp.where(stay, other, own)


def place_rows(me, own, other):
    return pl.pallas_call(
        rows_kernel,
        in_specs=[SCALARS] + [VECTORS] * 2,
        out_specs=VECTORS,
        out_shape=jax.ShapeDtypeStruct((128, own.shape[1]), bf16),
        compiler_params=pltpu.CompilerParams(vmem_limit_bytes=32 * MIB),
    )(me, own, other)


def tree_tables(lengths, parents, place):
    nseg = lengths.shape[1]
    batch = lengths.shape[0]
    ends = jnp.cumsum(lengths, axis=1)
    starts = ends - lengths
    segment = jnp.sum((place[None, :, None] >= ends[:, None, : nseg - 1]).astype(jnp.int32), axis=2)
    order = jnp.arange(nseg, dtype=jnp.int32)
    rows = [(order == 0).astype(f32)[None, :] * jnp.ones((batch, 1), f32)]
    depth = [jnp.zeros((batch,), jnp.int32)]
    for later in range(1, nseg):
        above = jnp.zeros_like(rows[0])
        reach = jnp.zeros_like(depth[0])
        for earlier in range(later):
            hit = parents[:, later] == earlier
            above = above + hit.astype(f32)[:, None] * rows[earlier]
            reach = reach + jnp.where(hit, depth[earlier] + lengths[:, earlier], 0)
        rows.append(above + (order == later).astype(f32)[None, :])
        depth.append(reach)
    ancestry = jnp.stack(rows, axis=1)
    begin = jnp.stack(depth, axis=1)
    pick = (segment[:, :, None] == order[None, None, :]).astype(f32)
    shift = (begin - starts).astype(f32)
    position = place[None, :].astype(f32) + jnp.sum(pick * shift[:, None, :], axis=2)
    linked = jnp.einsum("bis,bst,bjt->bij", pick, ancestry, pick)
    causal = place[None, :] <= place[:, None]
    return position, ((linked > 0.5) & causal[None]).astype(bf16)


def rotary_tables(position):
    half = HD // 2
    rates = jnp.exp(jnp.arange(half, dtype=f32) * (-2.0 * math.log(ROPE_BASE) / HD))
    angle = position[..., None] * rates
    cosine, sine = jnp.cos(angle), jnp.sin(angle)
    return jnp.concatenate([cosine, cosine], axis=-1), jnp.concatenate([-sine, sine], axis=-1)


def dot(left, right, contract):
    return lax.dot_general(
        left, right, (((contract[0],), (contract[1],)), ((), ())), preferred_element_type=f32
    )


def turn(value, cosine, sine):
    return value * cosine + pltpu.roll(value, HD // 2, 1) * sine


def attend_kernel(
    me_ref, x0_ref, x1_ref, x2_ref, x3_ref, w_ref, gain_ref, cos_ref, sin_ref, mask_ref,
    gains_out, n_ref, qkv_ref, mixed_ref, keep_ref, send_ref,
):
    gains = gain_ref[...].astype(f32).T[0:8, :]
    gains_out[...] = gains
    for k, x_ref in enumerate((x0_ref, x1_ref, x2_ref, x3_ref)):
        wide = x_ref[...].astype(f32)
        scale = lax.rsqrt(jnp.mean(wide * wide, axis=1, keepdims=True) + EPSILON)
        n_ref[k * 128 : k * 128 + 128, :] = (wide * scale * gains[0:1, :]).astype(bf16)
    joint = dot(n_ref[...], w_ref[:, 0:512], (1, 0))
    cosine, sine = cos_ref[0], sin_ref[0]
    keys = turn(joint[:, 256:384], cosine, sine).astype(bf16)
    values = joint[:, 384:512].astype(bf16)
    qkv_ref[:, 256:384] = keys
    qkv_ref[:, 384:512] = values
    allowed = mask_ref[0].astype(f32) > 0.5
    for head in range(2):
        at = slice(head * HD, head * HD + HD)
        queries = turn(joint[:, at], cosine, sine).astype(bf16)
        qkv_ref[:, at] = queries
        scores = dot(queries, keys, (1, 1)) * (1.0 / math.sqrt(HD))
        scores = jnp.where(allowed, scores, NEGATIVE)
        powers = jnp.exp(scores - jnp.max(scores, axis=1, keepdims=True))
        chance = (powers / jnp.sum(powers, axis=1, keepdims=True)).astype(bf16)
        mixed_ref[:, at] = dot(chance, values, (1, 0)).astype(bf16)
    part = dot(mixed_ref[...], w_ref[:, 512:768], (1, 1)).astype(bf16)
    keep_ref[...] = part[0:256]
    send_ref[...] = part[256:512]


def rows_of(mine, other):
    return mine, mine, other, other


ONCE = pl.Buffered(1)


def whole(shape):
    return pl.BlockSpec(shape, lambda i, me: (0,) * len(shape), pipeline_mode=ONCE)


ATTEND_COLUMNS = pl.BlockSpec((2048, 768), lambda i, me: (0, 0), pipeline_mode=ONCE)
GAIN_COLUMNS = pl.BlockSpec((2048, 128), lambda i, me: (0, 14), pipeline_mode=ONCE)


def attend(me, tokens, weights, cosine, sine, mask, tree):
    table = lambda width: pl.BlockSpec(
        (1, 512, width), lambda i, me: (tree, 0, 0), pipeline_mode=ONCE
    )
    shapes = [
        ((8, 2048), f32), ((512, 2048), bf16), ((512, 512), bf16), ((512, 256), bf16),
        ((256, 2048), bf16), ((256, 2048), bf16),
    ]
    return pl.pallas_call(
        attend_kernel,
        grid_spec=pltpu.PrefetchScalarGridSpec(
            num_scalar_prefetch=1,
            grid=(1,),
            in_specs=[
                pl.BlockSpec((128, 2048), lambda i, me, k=k: (k, 0), pipeline_mode=ONCE)
                for k in (0, 2)
            ]
            * 2
            + [ATTEND_COLUMNS, GAIN_COLUMNS, table(HD), table(HD), table(512)],
            out_specs=[whole(shape) for shape, _ in shapes],
        ),
        out_shape=[jax.ShapeDtypeStruct(shape, kind) for shape, kind in shapes],
        compiler_params=pltpu.CompilerParams(vmem_limit_bytes=(48 if tree else 36) * MIB),
        cost_estimate=COST,
    )(me, *rows_of(*tokens), weights, weights, cosine, sine, mask)


def attend_back_tree(branch_refs, w_ref, qkv_ref, cos_ref, sin_ref, mask_ref, keep_ref, send_ref,
                     js_ref):
    factor = 1.0 / math.sqrt(HD)
    mixed_slope = jnp.concatenate(
        [dot(ref[...], w_ref[:, 512:768], (1, 0)).astype(bf16) for ref in branch_refs], axis=0
    )
    cosine, sine = cos_ref[0], -sin_ref[0]
    allowed = mask_ref[0].astype(f32) > 0.5
    keys = qkv_ref[:, 256:384]
    values = qkv_ref[:, 384:512]
    key_slope = jnp.zeros((512, HD), f32)
    value_slope = jnp.zeros((512, HD), f32)
    for head in range(2):
        at = slice(head * HD, head * HD + HD)
        queries = qkv_ref[:, at]
        scores = jnp.where(allowed, dot(queries, keys, (1, 1)) * factor, NEGATIVE)
        powers = jnp.exp(scores - jnp.max(scores, axis=1, keepdims=True))
        chance = powers / jnp.sum(powers, axis=1, keepdims=True)
        slope = mixed_slope[:, at]
        value_slope += dot(chance.astype(bf16), slope, (0, 0))
        chance_slope = dot(slope, values, (1, 1))
        balance = jnp.sum(chance * chance_slope, axis=1, keepdims=True)
        score_slope = (chance * (chance_slope - balance)).astype(bf16)
        query_slope = dot(score_slope, keys, (1, 0)) * factor
        js_ref[:, at] = turn(query_slope, cosine, sine).astype(bf16)
        key_slope += dot(score_slope, queries, (0, 0)) * factor
    js_ref[:, 256:384] = turn(key_slope, cosine, sine).astype(bf16)
    js_ref[:, 384:512] = value_slope.astype(bf16)
    part = dot(js_ref[...], w_ref[:, 0:512], (1, 1)).astype(bf16)
    keep_ref[...] = part[0:256]
    send_ref[...] = part[256:512]


def attend_back_first_kernel(
    me_ref, b0_ref, b1_ref, w_ref, qkv_ref, cos_ref, sin_ref, mask_ref, keep_ref, send_ref, js_ref
):
    attend_back_tree(
        (b0_ref, b1_ref), w_ref, qkv_ref, cos_ref, sin_ref, mask_ref, keep_ref, send_ref, js_ref
    )


def attend_back_second_kernel(
    me_ref, b0_ref, b1_ref, w_ref, qkv_ref, cos_ref, sin_ref, mask_ref,
    other0_ref, other1_ref, other_js, n0_ref, n1_ref, mixed0_ref, mixed1_ref, *refs,
):
    keep_ref, send_ref = refs[0:2]
    stay_refs, go_refs = refs[2:4], refs[4:6]
    js_ref, joint_acc, mixing_acc = refs[6:9]
    z, y = me_ref[0], me_ref[1]
    attend_back_tree(
        (b0_ref, b1_ref), w_ref, qkv_ref, cos_ref, sin_ref, mask_ref, keep_ref, send_ref, js_ref
    )
    joint_acc[...] = dot(n0_ref[...], other_js[...], (0, 0)) + dot(n1_ref[...], js_ref[...], (0, 0))
    mixing_acc[...] = (
        dot(other0_ref[...], mixed0_ref[0:256, :], (0, 0))
        + dot(other1_ref[...], mixed0_ref[256:512, :], (0, 0))
        + dot(b0_ref[...], mixed1_ref[0:256, :], (0, 0))
        + dot(b1_ref[...], mixed1_ref[256:512, :], (0, 0))
    )
    for stream in range(2):
        order = stream_order(stream)
        for i in range(4):
            for j in range(4):
                dz, dy = (order[i], order[j]) if stream == 0 else (order[j], order[i])
                first = ((z ^ dz) * 4 + (y ^ dy)) * 128 + stream * 64
                rows = pl.ds(pl.multiple_of(first, 64), 64)
                out = stay_refs[stream] if i < 2 else go_refs[stream]
                out[i % 2, j, :, 0:512] = joint_acc[rows, :].astype(bf16)
                out[i % 2, j, :, 512:768] = mixing_acc[rows, :].astype(bf16)


def attend_back(me, branch, weights, qkv, cosine, sine, mask, tree, others=None):
    table = lambda width: pl.BlockSpec(
        (1, 512, width), lambda i, me: (tree, 0, 0), pipeline_mode=ONCE
    )
    part = ((256, 2048), bf16)
    shapes = [part, part]
    scratch = []
    if others is None:
        shapes.append(((512, 512), bf16))
    else:
        shapes += [((2, 4, 64, 768), bf16)] * 4
        scratch = [
            pltpu.VMEM((512, 512), bf16), pltpu.VMEM((2048, 512), f32), pltpu.VMEM((2048, 256), f32)
        ]
    extra = () if others is None else others
    return pl.pallas_call(
        attend_back_first_kernel if others is None else attend_back_second_kernel,
        grid_spec=pltpu.PrefetchScalarGridSpec(
            num_scalar_prefetch=1,
            grid=(1,),
            in_specs=[whole((256, 2048))] * 2 + [ATTEND_COLUMNS, whole((512, 512))]
            + [table(HD), table(HD), table(512)]
            + [whole(item.shape) for item in extra],
            out_specs=[whole(shape) for shape, _ in shapes],
            scratch_shapes=scratch,
        ),
        out_shape=[jax.ShapeDtypeStruct(shape, kind) for shape, kind in shapes],
        compiler_params=pltpu.CompilerParams(vmem_limit_bytes=(36 if others is None else 48) * MIB),
        cost_estimate=COST,
    )(me, *branch, weights, qkv, cosine, sine, mask, *extra)


SLOPE_CHUNKS = [pl.BlockSpec((128, 2048), lambda j, k=k: (k, 0)) for k in (1, 3)] * 2


def hidden_slope_kernel(*refs):
    x_refs, w_ref, o_ref, whole_ref = refs[:8], refs[8], refs[9], refs[10]

    @pl.when(pl.program_id(0) == 0)
    def _():
        for k in range(8):
            whole_ref[k * 128 : k * 128 + 128, :] = x_refs[k][...]

    o_ref[...] = dot(whole_ref[...], w_ref[...], (1, 0))


def hidden_slopes(feed0, feed1, weights):
    return pl.pallas_call(
        hidden_slope_kernel,
        grid=(4,),
        in_specs=SLOPE_CHUNKS * 2 + [pl.BlockSpec((2048, 256), lambda j: (0, j + 3))],
        out_specs=pl.BlockSpec((1024, 256), lambda j: (0, j)),
        out_shape=jax.ShapeDtypeStruct((1024, 1024), f32),
        scratch_shapes=[pltpu.VMEM((1024, 2048), bf16)],
        compiler_params=pltpu.CompilerParams(vmem_limit_bytes=48 * MIB),
        cost_estimate=COST,
    )(*rows_of(*feed0), *rows_of(*feed1), weights)


def feed_kernel(*refs):
    n_refs, gate_ref, up_ref, slope_ref, out0_ref, out1_ref, whole_ref = refs[:4], *refs[4:]

    @pl.when(pl.program_id(0) == 0)
    def _():
        for k in range(4):
            whole_ref[k * 256 : k * 256 + 256, :] = n_refs[k][...]

    for tree, out_ref in enumerate((out0_ref, out1_ref)):
        rows = slice(tree * 512, tree * 512 + 512)
        gate = dot(whole_ref[rows, :], gate_ref[...], (1, 0))
        upper = dot(whole_ref[rows, :], up_ref[...], (1, 0))
        slope = slope_ref[tree * 512 : tree * 512 + 512, :]
        sigma = jax.nn.sigmoid(gate)
        active = gate * sigma
        out_ref[0] = (slope * upper * sigma * (1.0 + gate * (1.0 - sigma))).astype(bf16)
        out_ref[1] = (slope * active).astype(bf16)
        out_ref[2] = (active * upper).astype(bf16)


def feed_forward(normed, weights, slopes):
    return pl.pallas_call(
        feed_kernel,
        grid=(4,),
        in_specs=[pl.BlockSpec((256, 2048), lambda j: (0, 0))] * 4
        + [
            pl.BlockSpec((2048, 256), lambda j: (0, j)),
            pl.BlockSpec((2048, 256), lambda j: (0, j + 4)),
            pl.BlockSpec((1024, 256), lambda j: (0, j)),
        ],
        out_specs=[pl.BlockSpec((3, 512, 256), lambda j: (0, 0, j))] * 2,
        out_shape=(jax.ShapeDtypeStruct((3, 512, 1024), bf16),) * 2,
        scratch_shapes=[pltpu.VMEM((1024, 2048), bf16)],
        compiler_params=pltpu.CompilerParams(vmem_limit_bytes=48 * MIB),
        cost_estimate=COST,
    )(*normed, weights, weights, slopes)


def feed_grad_kernel(*refs):
    n_refs, f_refs = refs[0:4], refs[4:12]
    s0_ref, s1_ref, out_ref, turned = refs[12:16]
    step = pl.program_id(0)

    @pl.when(step == 0)
    def _():
        for k in range(4):
            turned[:, k * 256 : k * 256 + 256] = n_refs[k][...].T

    @pl.when(step == 8)
    def _():
        for k in range(8):
            turned[:, k * 128 : k * 128 + 128] = f_refs[k][...].T

    slopes = jnp.concatenate([s0_ref[0], s1_ref[0]], axis=0)
    out_ref[...] = dot(turned[...], slopes, (1, 0)).astype(bf16)


def feed_grads(normed, feed0, feed1, slopes):
    return pl.pallas_call(
        feed_grad_kernel,
        grid=(12,),
        in_specs=[pl.BlockSpec((256, 2048), lambda j: (0, 0))] * 4
        + SLOPE_CHUNKS * 2
        + [pl.BlockSpec((1, 512, 256), lambda j: (j // 4, 0, j % 4))] * 2,
        out_specs=pl.BlockSpec((2048, 256), lambda j: (0, j)),
        out_shape=jax.ShapeDtypeStruct((2048, 3072), bf16),
        scratch_shapes=[pltpu.VMEM((2048, 1024), bf16)],
        compiler_params=pltpu.CompilerParams(vmem_limit_bytes=48 * MIB),
        cost_estimate=COST,
    )(*normed, *rows_of(*feed0), *rows_of(*feed1), *slopes)


def split_rows(part, keep_ref, send_ref):
    keep_ref[...] = part[0:256]
    send_ref[...] = part[256:512]


def normed_slope_kernel(g_ref, u_ref, wg_ref, wu_ref, keep_ref, send_ref):
    part = dot(g_ref[0], wg_ref[...], (1, 1)) + dot(u_ref[0], wu_ref[...], (1, 1))
    split_rows(part.astype(bf16), keep_ref, send_ref)


def normed_slopes(slopes, weights, tree):
    half = jax.ShapeDtypeStruct((256, 2048), bf16)
    return pl.pallas_call(
        normed_slope_kernel,
        grid=(4,),
        in_specs=[
            pl.BlockSpec((1, 512, 1024), lambda j: (0, 0, 0), pipeline_mode=ONCE),
            pl.BlockSpec((1, 512, 1024), lambda j: (1, 0, 0), pipeline_mode=ONCE),
            pl.BlockSpec((512, 1024), lambda j: (j, 0)),
            pl.BlockSpec((512, 1024), lambda j: (j, 1)),
        ],
        out_specs=[pl.BlockSpec((256, 512), lambda j: (0, j))] * 2,
        out_shape=(half, half),
        compiler_params=pltpu.CompilerParams(vmem_limit_bytes=(20 if tree else 48) * MIB),
        cost_estimate=COST,
    )(slopes, slopes, weights, weights)


def down_kernel(h_ref, w0, w1, w2, w3, keep_ref, send_ref):
    weights = jnp.concatenate([w0[...], w1[...], w2[...], w3[...]], axis=1)
    split_rows(dot(h_ref[0], weights, (1, 1)).astype(bf16), keep_ref, send_ref)


def down(slopes, weights):
    half = jax.ShapeDtypeStruct((256, 2048), bf16)
    return pl.pallas_call(
        down_kernel,
        grid=(4,),
        in_specs=[
            pl.BlockSpec((1, 512, 1024), lambda j: (2, 0, 0)),
            pl.BlockSpec((512, 256), lambda j: (j, 3)),
            pl.BlockSpec((512, 256), lambda j: (j, 4)),
            pl.BlockSpec((512, 256), lambda j: (j, 5)),
            pl.BlockSpec((512, 256), lambda j: (j, 6)),
        ],
        out_specs=[pl.BlockSpec((256, 512), lambda j: (0, j))] * 2,
        out_shape=(half, half),
        compiler_params=pltpu.CompilerParams(vmem_limit_bytes=48 * MIB),
        cost_estimate=COST,
    )(slopes, *([weights] * 4))


def norm_back(slope, incoming, scale, gain):
    weighted = slope * gain
    cubed = scale * scale * scale
    return scale * weighted - incoming * cubed * jnp.mean(weighted * incoming, axis=1, keepdims=True)


def shards(
    tokens, attend_gain, joint_weight, mixing_weight, feed_gain, gate_weight, up_weight,
    down_weight, lengths, parents, cotangent,
):
    z, y = lax.axis_index("z"), lax.axis_index("y")
    xh, xl, core = lax.axis_index("xh"), lax.axis_index("xl"), lax.axis_index("core")
    me = jnp.stack([z, y, xh * 4 + xl * 2 + core, xh]).astype(jnp.int32)

    def home_start(total):
        rows = total.shape[0] // 2
        own = jnp.where(xh == 0, total[:rows], total[rows:])
        return own, team_swap(jnp.where(xh == 0, total[rows:], total[:rows]), 1, 0, 0)

    def home_end(own, other, widths):
        first = jnp.where(xh == 0, own, other).astype(f32)
        second = jnp.where(xh == 0, other, own).astype(f32)
        out, at = [], 0
        for width in widths:
            out.append(
                jnp.concatenate([first[:, at : at + width], second[:, at : at + width]], axis=1)
            )
            at += width
        return out

    gains = jnp.concatenate([attend_gain, feed_gain])[None]
    own, send = prepare_weights(
        prepare_attend_kernel, me, 1920, joint_weight, mixing_weight.T, down_weight.T, gains
    )
    other = team_swap(send, 1, 0, 0)
    trees = jnp.concatenate([lengths, parents], axis=0)
    other, trees_other = after((other, team_swap(trees, 1, 0, 0)))
    own_rows, cotangent_own = prepare_rows(tokens[:, 0], after(cotangent[:, 0], send))
    attend_rows = place_rows(me, own, other)
    weights = lax.all_gather(attend_rows, GRID, axis=0, tiled=True)

    rows_started = gather_start(after(own_rows, attend_rows))
    feed_stay, feed_send = prepare_weights(
        prepare_feed_kernel, me, 2048, gate_weight, after(up_weight, attend_rows)
    )
    trees = jnp.stack([trees, trees_other])
    chunk = jnp.arange(4, dtype=jnp.int32)
    place = ((xl ^ (chunk % 2)) * 2 + (core ^ (chunk // 2))) * 128
    place = (place[:, None] + jnp.arange(128, dtype=jnp.int32)[None]).reshape(512)
    position, mask = tree_tables(trees[:, 0], trees[:, 1], place)
    cosine, sine = rotary_tables(position)
    rows_started, mask, cosine, sine, feed_send = after(
        (rows_started, mask, cosine, sine, feed_send)
    )
    rows_later = gather_next(own_rows, rows_started)
    feed_other = team_swap(feed_send, 1, 0, 0)
    rows_later, feed_other = after((rows_later, feed_other))
    feed_rows = place_rows(me, feed_stay, feed_other)
    feed_weights = lax.all_gather(feed_rows, GRID, axis=0, tiled=True)
    rows0 = gather_first(rows_later)
    rows1 = gather_second(rows_started, rows_later)
    rows0, rows1, feed_rows, weights = after((rows0, rows1, feed_rows, weights))

    gains, normed1, qkv1, mixed1, *part1 = attend(me, rows1, weights, cosine, sine, mask, 1)
    sums1 = scatter_sums(scatter_start(part1), 1)
    terms1 = scatter_next(sums1, 1)
    _, normed0, qkv0, mixed0, *part0 = attend(
        me, after(rows0, sums1), weights, cosine, sine, mask, 0
    )
    sums0 = scatter_sums(scatter_start(part0), 0)
    terms0 = scatter_next(sums0, 0)
    hidden_slope = hidden_slopes(after(rows0, sums0), rows1, weights)
    terms0, terms1, hidden_slope = after((terms0, terms1, hidden_slope))
    gain_one, gain_two = gains[0:1], gains[1:2]
    incoming = own_rows[:128].astype(f32)
    middle = incoming + total(terms0 + terms1)
    scale_two = lax.rsqrt(jnp.mean(middle * middle, axis=1, keepdims=True) + EPSILON)
    low = (middle * scale_two * gain_two).astype(bf16)
    started = gather_start(low)
    later = gather_next(low, started)
    two = gather_first(later) + gather_second(started, later)

    slopes0, slopes1 = feed_forward(two, feed_weights, hidden_slope)
    sums1 = scatter_sums(scatter_start(normed_slopes(slopes1, feed_weights, 1)), 1)
    terms1 = scatter_next(sums1, 1)
    feed_grad = feed_grads(two, rows0, rows1, after((slopes0, slopes1), sums1))
    terms1, feed_grad = after((terms1, feed_grad))
    feed_sum = lax.psum_scatter(feed_grad, GRID, scatter_dimension=0, tiled=True)
    sums0 = scatter_sums(scatter_start(normed_slopes(after(slopes0, feed_grad), feed_weights, 0)), 0)
    terms0 = scatter_next(sums0, 0)
    down0 = down(after(slopes0, sums0), weights)
    down1 = down(after(slopes1, sums0), weights)
    terms0, down0, down1 = after((terms0, down0, down1))

    middle_slope = cotangent_own + norm_back(
        total(terms0 + terms1), middle, scale_two, gain_two
    )
    low = middle_slope.astype(bf16)
    started = gather_start(low)
    down0, down1 = after((down0, down1), low)
    down0 = scatter_sums(scatter_start(down0), 0)
    down1 = scatter_sums(scatter_start(down1), 1)
    started, down0, down1 = after((started, down0, down1))
    later = gather_next(low, started)
    branch0 = gather_first(later)
    keep0, send0, js0 = attend_back(me, branch0, weights, qkv0, cosine, sine, mask, 0)
    branch1 = gather_second(started, later)

    sums0 = scatter_sums(scatter_start((keep0, send0)), 0)
    input_terms0 = scatter_next(sums0, 0)
    keep1, send1, *streams = attend_back(
        me, after(branch1, js0, sums0), weights, qkv1, cosine, sine, mask, 1,
        (*branch0, js0, normed0, normed1, mixed0, mixed1),
    )

    input_terms1 = scatter_next(scatter_sums(scatter_start((keep1, send1)), 1), 1)
    feed_own, feed_other = home_start(feed_sum)
    down_terms = scatter_next(after(down0, input_terms0), 0) + scatter_next(
        after(down1, input_terms0), 1
    )
    attend_sum, (input_terms0, input_terms1), (down_terms, feed_other) = grid_scatter(
        streams[:2], streams[2:], (input_terms0, input_terms1), (down_terms, feed_other)
    )
    layer_output = middle + total(down_terms)
    attend_own, attend_other = home_start(attend_sum)
    scale_one = lax.rsqrt(jnp.mean(incoming * incoming, axis=1, keepdims=True) + EPSILON)
    input_gradient = middle_slope + norm_back(
        total(input_terms0 + input_terms1), incoming, scale_one, gain_one
    )
    gate_grad, up_grad, down_grad = home_end(feed_own, feed_other, (1024, 1024, 1024))
    joint_grad, mixing_grad = home_end(attend_own, attend_other, (512, 256))

    attend_part = jnp.sum(joint_weight.astype(f32) * joint_grad, axis=1)
    feed_part = jnp.sum(
        gate_weight.astype(f32) * gate_grad + up_weight.astype(f32) * up_grad, axis=1
    )
    attend_total, feed_total = lax.psum((attend_part, feed_part), ("xl", "core"))
    return (
        lane_back(layer_output)[:, None],
        lane_back(input_gradient)[:, None],
        attend_total / attend_gain.astype(f32),
        joint_grad,
        mixing_grad.T,
        feed_total / feed_gain.astype(f32),
        gate_grad,
        up_grad,
        down_grad.T,
    )


def solution(mesh):
    fine = Mesh(mesh.devices.reshape(4, 2, 4, 2, 2), ("z", "xh", "y", "xl", "core"))
    fsdp = ("z", "xh", "y")
    tensor = ("xl", "core")
    in_specs = (
        P(tensor, fsdp, None),
        P(fsdp),
        P(fsdp, tensor),
        P(tensor, fsdp),
        P(fsdp),
        P(fsdp, tensor),
        P(fsdp, tensor),
        P(tensor, fsdp),
        P(fsdp, None),
        P(fsdp, None),
        P(tensor, fsdp, None),
    )
    out_specs = (
        P(tensor, fsdp, None),
        P(tensor, fsdp, None),
        P(fsdp),
        P(fsdp, tensor),
        P(tensor, fsdp),
        P(fsdp),
        P(fsdp, tensor),
        P(fsdp, tensor),
        P(tensor, fsdp),
    )
    return jax.shard_map(shards, mesh=fine, in_specs=in_specs, out_specs=out_specs, check_vma=False)
```

```python
import math

import jax
import jax.numpy as jnp
from jax import lax
from jax.experimental import pallas as pl
from jax.experimental.pallas import tpu as pltpu
from jax.sharding import Mesh
from jax.sharding import PartitionSpec as P

HEADS = 16
KVH = 8
HD = 128
EPSILON = 1e-06
ROPE_BASE = 1000000.0
NEGATIVE = -1e30
MIB = 1024 * 1024
COST = pl.CostEstimate(flops=1 << 20, bytes_accessed=1 << 17, transcendentals=0)

TEAM = ("xh", "xl", "core")
GRID = ("z", "y")

bf16 = jnp.bfloat16
f32 = jnp.float32


def team_swap(value, a, b, c):
    flip = a * 4 + b * 2 + c
    with jax.named_scope(f"team_{a}{b}{c}"):
        return lax.ppermute(value, TEAM, [(i, i ^ flip) for i in range(8)])


def axis_swap(value, axis, flip):
    with jax.named_scope(f"grid_{axis}{flip}"):
        return lax.ppermute(value, axis, [(i, i ^ flip) for i in range(4)])


def after(value, *others):
    return lax.optimization_barrier((value, others))[0]


@jax.named_scope("gather_start")
def gather_start(own):
    return team_swap(own, 0, 1, 0), team_swap(own, 1, 1, 0)


@jax.named_scope("gather_next")
def gather_next(own, started):
    near, next_ = started
    half = near.shape[0] // 2
    pair = jnp.concatenate([own, near], axis=0)
    return (
        pair,
        team_swap(near[:half], 1, 1, 0),
        team_swap(next_[half:], 0, 1, 0),
        team_swap(pair, 0, 0, 1),
    )


def gather_first(later):
    return later[0], later[3]


@jax.named_scope("gather_end")
def gather_second(started, later):
    pair = jnp.concatenate([later[1], later[2], started[1]], axis=0)
    return pair, team_swap(pair, 0, 0, 1)


@jax.named_scope("scatter_start")
def scatter_start(part):
    keep, send = part
    return keep, team_swap(send, 0, 0, 1)


def scatter_sums(started, tree):
    keep, got = started
    low = keep[:128].astype(f32) + got[:128].astype(f32)
    high = (keep[128:].astype(f32) + got[128:].astype(f32)).astype(bf16)
    return (low.astype(bf16) if tree else low), high


@jax.named_scope("scatter_next")
def scatter_next(sums, tree):
    low, high = sums
    if tree == 0:
        return low, team_swap(high, 0, 1, 0)
    return team_swap(low, 1, 0, 0), team_swap(high, 1, 1, 0)


def total(terms):
    return sum((item.astype(f32) for item in terms[1:]), terms[0].astype(f32))


STREAMS = (("z", 1, 3), ("y", 1, 3))


def stream_order(stream):
    _, first, second = STREAMS[stream]
    return (0, second, first, 2)


def stream_swap(values, step):
    out = []
    for (axis, first, second), value in zip(STREAMS, values):
        if step >= 2:
            axis = "y" if axis == "z" else "z"
        out.append(axis_swap(value, axis, second if step % 2 else first))
    return out


def add_kernel(*refs):
    count = len(refs) // 4
    for i in range(count):
        total = refs[i][...].astype(f32) + refs[count + i][...].astype(f32)
        low = total.astype(bf16)
        half = low.shape[0] // 2
        refs[2 * count + i][...] = low[:half]
        refs[3 * count + i][...] = low[half:]


def add_streams(stay, came):
    half = jax.ShapeDtypeStruct((stay[0].shape[0] // 2,) + stay[0].shape[1:], bf16)
    out = pl.pallas_call(
        add_kernel,
        out_shape=(half,) * (2 * len(stay)),
        compiler_params=pltpu.CompilerParams(vmem_limit_bytes=24 * MIB),
    )(*stay, *came)
    return out[: len(stay)], out[len(stay) :]


def add_blocks_kernel(*refs):
    count = len(refs) // 6
    for i in range(count):
        low = (refs[i][...].astype(f32) + refs[count + i][...].astype(f32)).astype(bf16)
        for k in range(4):
            refs[2 * count + 4 * i + k][...] = low[k]


def add_blocks(stay, came):
    out = pl.pallas_call(
        add_blocks_kernel,
        out_shape=(jax.ShapeDtypeStruct(stay[0].shape[1:], bf16),) * (4 * len(stay)),
        compiler_params=pltpu.CompilerParams(vmem_limit_bytes=24 * MIB),
    )(*stay, *came)
    return [out[4 * i : 4 * i + 4] for i in range(len(stay))]


def grid_scatter(stay, go, first, second):
    came, first = after((stream_swap(go, 0), first))
    stay, go = add_streams(stay, came)
    came, second = after((stream_swap(go, 1), second))
    parts = add_blocks(
        [value.reshape(4, 64, 768) for value in stay], [value.reshape(4, 64, 768) for value in came]
    )
    came = []
    for stream, part in enumerate(parts):
        axis = "y" if STREAMS[stream][0] == "z" else "z"
        order = stream_order(stream)
        came.append([axis_swap(part[k], axis, order[k]) for k in (1, 2, 3)])
    came = after(came)
    rows = [
        sum((item.astype(f32) for item in got), part[0].astype(f32)).astype(bf16)
        for part, got in zip(parts, came)
    ]
    return jnp.concatenate(rows, axis=0), first, second


def lane_order(value):
    parts = []
    for z in range(4):
        for y in range(4):
            for xh in range(2):
                start = z * 512 + xh * 256 + y * 64
                parts.append(value[:, start : start + 64])
    return jnp.concatenate(parts, axis=1)


def lane_back(value):
    parts = []
    for z in range(4):
        for xh in range(2):
            for y in range(4):
                start = z * 512 + y * 128 + xh * 64
                parts.append(value[:, start : start + 64])
    return jnp.concatenate(parts, axis=1)


SCALARS = pl.BlockSpec(memory_space=pltpu.SMEM)
VECTORS = pl.BlockSpec(memory_space=pltpu.VMEM)


def put_halves(value, at, stay, own_ref, send_ref):
    half = value.shape[1] // 2
    first, second = value[:, :half], value[:, half:]
    own_ref[:, at : at + half] = jnp.where(stay, first, second)
    send_ref[:, at : at + half] = jnp.where(stay, second, first)


def prepare_attend_kernel(me_ref, joint_ref, mixing_ref, down_ref, gain_ref, own_ref, send_ref):
    stay = me_ref[3] == 0
    put_halves(joint_ref[...], 0, stay, own_ref, send_ref)
    put_halves(mixing_ref[...], 512, stay, own_ref, send_ref)
    put_halves(down_ref[...], 768, stay, own_ref, send_ref)
    gains = jnp.broadcast_to(gain_ref[...].astype(f32), (128, 128)).T
    lane = lax.broadcasted_iota(jnp.int32, (64, 128), 1)
    gains = jnp.where(lane == 0, gains[0:64], gains[64:128]).astype(bf16)
    own_ref[:, 1792:1920] = gains
    send_ref[:, 1792:1920] = gains


def prepare_feed_kernel(me_ref, gate_ref, up_ref, own_ref, send_ref):
    stay = me_ref[3] == 0
    put_halves(gate_ref[...], 0, stay, own_ref, send_ref)
    put_halves(up_ref[...], 1024, stay, own_ref, send_ref)


def prepare_weights(kernel, me, width, *values):
    return pl.pallas_call(
        kernel,
        in_specs=[SCALARS] + [VECTORS] * len(values),
        out_specs=[VECTORS] * 2,
        out_shape=(jax.ShapeDtypeStruct((64, width), bf16),) * 2,
        compiler_params=pltpu.CompilerParams(vmem_limit_bytes=32 * MIB),
    )(me, *values)


def prepare_rows_kernel(tokens_ref, slope_ref, rows_out, slope_out):
    rows_out[0:128, :] = lane_order(tokens_ref[...].astype(f32)).astype(bf16)
    slope = lane_order(slope_ref[...])
    slope_out[...] = slope
    rows_out[128:256, :] = slope.astype(bf16)


def prepare_rows(tokens, slope):
    return pl.pallas_call(
        prepare_rows_kernel,
        out_shape=(
            jax.ShapeDtypeStruct((256, 2048), bf16),
            jax.ShapeDtypeStruct(slope.shape, f32),
        ),
        compiler_params=pltpu.CompilerParams(vmem_limit_bytes=32 * MIB),
    )(tokens, slope)


def rows_kernel(me_ref, own_ref, other_ref, out_ref):
    stay = me_ref[3] == 0
    own, other = own_ref[...], other_ref[...]
    out_ref[0:64, :] = jnp.where(stay, own, other)
    out_ref[64:128, :] = jnp.where(stay, other, own)


def place_rows(me, own, other):
    return pl.pallas_call(
        rows_kernel,
        in_specs=[SCALARS] + [VECTORS] * 2,
        out_specs=VECTORS,
        out_shape=jax.ShapeDtypeStruct((128, own.shape[1]), bf16),
        compiler_params=pltpu.CompilerParams(vmem_limit_bytes=32 * MIB),
    )(me, own, other)


def tree_tables(lengths, parents, place):
    nseg = lengths.shape[1]
    batch = lengths.shape[0]
    ends = jnp.cumsum(lengths, axis=1)
    starts = ends - lengths
    segment = jnp.sum((place[None, :, None] >= ends[:, None, : nseg - 1]).astype(jnp.int32), axis=2)
    order = jnp.arange(nseg, dtype=jnp.int32)
    rows = [(order == 0).astype(f32)[None, :] * jnp.ones((batch, 1), f32)]
    depth = [jnp.zeros((batch,), jnp.int32)]
    for later in range(1, nseg):
        above = jnp.zeros_like(rows[0])
        reach = jnp.zeros_like(depth[0])
        for earlier in range(later):
            hit = parents[:, later] == earlier
            above = above + hit.astype(f32)[:, None] * rows[earlier]
            reach = reach + jnp.where(hit, depth[earlier] + lengths[:, earlier], 0)
        rows.append(above + (order == later).astype(f32)[None, :])
        depth.append(reach)
    ancestry = jnp.stack(rows, axis=1)
    begin = jnp.stack(depth, axis=1)
    pick = (segment[:, :, None] == order[None, None, :]).astype(f32)
    shift = (begin - starts).astype(f32)
    position = place[None, :].astype(f32) + jnp.sum(pick * shift[:, None, :], axis=2)
    linked = jnp.einsum("bis,bst,bjt->bij", pick, ancestry, pick)
    causal = place[None, :] <= place[:, None]
    return position, ((linked > 0.5) & causal[None]).astype(bf16)


def rotary_tables(position):
    half = HD // 2
    rates = jnp.exp(jnp.arange(half, dtype=f32) * (-2.0 * math.log(ROPE_BASE) / HD))
    angle = position[..., None] * rates
    cosine, sine = jnp.cos(angle), jnp.sin(angle)
    return jnp.concatenate([cosine, cosine], axis=-1), jnp.concatenate([-sine, sine], axis=-1)


def dot(left, right, contract):
    return lax.dot_general(
        left, right, (((contract[0],), (contract[1],)), ((), ())), preferred_element_type=f32
    )


def turn(value, cosine, sine):
    return value * cosine + pltpu.roll(value, HD // 2, 1) * sine


def attend_kernel(
    me_ref, x0_ref, x1_ref, x2_ref, x3_ref, w_ref, gain_ref, cos_ref, sin_ref, mask_ref,
    gains_out, n_ref, qkv_ref, mixed_ref, keep_ref, send_ref,
):
    gains = gain_ref[...].astype(f32).T[0:8, :]
    gains_out[...] = gains
    for k, x_ref in enumerate((x0_ref, x1_ref, x2_ref, x3_ref)):
        wide = x_ref[...].astype(f32)
        scale = lax.rsqrt(jnp.mean(wide * wide, axis=1, keepdims=True) + EPSILON)
        n_ref[k * 128 : k * 128 + 128, :] = (wide * scale * gains[0:1, :]).astype(bf16)
    joint = dot(n_ref[...], w_ref[:, 0:512], (1, 0))
    cosine, sine = cos_ref[0], sin_ref[0]
    keys = turn(joint[:, 256:384], cosine, sine).astype(bf16)
    values = joint[:, 384:512].astype(bf16)
    qkv_ref[:, 256:384] = keys
    qkv_ref[:, 384:512] = values
    allowed = mask_ref[0].astype(f32) > 0.5
    for head in range(2):
        at = slice(head * HD, head * HD + HD)
        queries = turn(joint[:, at], cosine, sine).astype(bf16)
        qkv_ref[:, at] = queries
        scores = dot(queries, keys, (1, 1)) * (1.0 / math.sqrt(HD))
        scores = jnp.where(allowed, scores, NEGATIVE)
        powers = jnp.exp(scores - jnp.max(scores, axis=1, keepdims=True))
        chance = (powers / jnp.sum(powers, axis=1, keepdims=True)).astype(bf16)
        mixed_ref[:, at] = dot(chance, values, (1, 0)).astype(bf16)
    part = dot(mixed_ref[...], w_ref[:, 512:768], (1, 1)).astype(bf16)
    keep_ref[...] = part[0:256]
    send_ref[...] = part[256:512]


def rows_of(mine, other):
    return mine, mine, other, other


ONCE = pl.Buffered(1)


def whole(shape):
    return pl.BlockSpec(shape, lambda i, me: (0,) * len(shape), pipeline_mode=ONCE)


ATTEND_COLUMNS = pl.BlockSpec((2048, 768), lambda i, me: (0, 0), pipeline_mode=ONCE)
GAIN_COLUMNS = pl.BlockSpec((2048, 128), lambda i, me: (0, 14), pipeline_mode=ONCE)


def attend(me, tokens, weights, cosine, sine, mask, tree):
    table = lambda width: pl.BlockSpec(
        (1, 512, width), lambda i, me: (tree, 0, 0), pipeline_mode=ONCE
    )
    shapes = [
        ((8, 2048), f32), ((512, 2048), bf16), ((512, 512), bf16), ((512, 256), bf16),
        ((256, 2048), bf16), ((256, 2048), bf16),
    ]
    return pl.pallas_call(
        attend_kernel,
        grid_spec=pltpu.PrefetchScalarGridSpec(
            num_scalar_prefetch=1,
            grid=(1,),
            in_specs=[
                pl.BlockSpec((128, 2048), lambda i, me, k=k: (k, 0), pipeline_mode=ONCE)
                for k in (0, 2)
            ]
            * 2
            + [ATTEND_COLUMNS, GAIN_COLUMNS, table(HD), table(HD), table(512)],
            out_specs=[whole(shape) for shape, _ in shapes],
        ),
        out_shape=[jax.ShapeDtypeStruct(shape, kind) for shape, kind in shapes],
        compiler_params=pltpu.CompilerParams(vmem_limit_bytes=(48 if tree else 36) * MIB),
        cost_estimate=COST,
    )(me, *rows_of(*tokens), weights, weights, cosine, sine, mask)


def attend_back_tree(branch_refs, w_ref, qkv_ref, cos_ref, sin_ref, mask_ref, keep_ref, send_ref,
                     js_ref):
    factor = 1.0 / math.sqrt(HD)
    mixed_slope = jnp.concatenate(
        [dot(ref[...], w_ref[:, 512:768], (1, 0)).astype(bf16) for ref in branch_refs], axis=0
    )
    cosine, sine = cos_ref[0], -sin_ref[0]
    allowed = mask_ref[0].astype(f32) > 0.5
    keys = qkv_ref[:, 256:384]
    values = qkv_ref[:, 384:512]
    key_slope = jnp.zeros((512, HD), f32)
    value_slope = jnp.zeros((512, HD), f32)
    for head in range(2):
        at = slice(head * HD, head * HD + HD)
        queries = qkv_ref[:, at]
        scores = jnp.where(allowed, dot(queries, keys, (1, 1)) * factor, NEGATIVE)
        powers = jnp.exp(scores - jnp.max(scores, axis=1, keepdims=True))
        chance = powers / jnp.sum(powers, axis=1, keepdims=True)
        slope = mixed_slope[:, at]
        value_slope += dot(chance.astype(bf16), slope, (0, 0))
        chance_slope = dot(slope, values, (1, 1))
        balance = jnp.sum(chance * chance_slope, axis=1, keepdims=True)
        score_slope = (chance * (chance_slope - balance)).astype(bf16)
        query_slope = dot(score_slope, keys, (1, 0)) * factor
        js_ref[:, at] = turn(query_slope, cosine, sine).astype(bf16)
        key_slope += dot(score_slope, queries, (0, 0)) * factor
    js_ref[:, 256:384] = turn(key_slope, cosine, sine).astype(bf16)
    js_ref[:, 384:512] = value_slope.astype(bf16)
    part = dot(js_ref[...], w_ref[:, 0:512], (1, 1)).astype(bf16)
    keep_ref[...] = part[0:256]
    send_ref[...] = part[256:512]


def attend_back_first_kernel(
    me_ref, b0_ref, b1_ref, w_ref, qkv_ref, cos_ref, sin_ref, mask_ref, keep_ref, send_ref, js_ref
):
    attend_back_tree(
        (b0_ref, b1_ref), w_ref, qkv_ref, cos_ref, sin_ref, mask_ref, keep_ref, send_ref, js_ref
    )


def attend_back_second_kernel(
    me_ref, b0_ref, b1_ref, w_ref, qkv_ref, cos_ref, sin_ref, mask_ref,
    other0_ref, other1_ref, other_js, n0_ref, n1_ref, mixed0_ref, mixed1_ref, *refs,
):
    keep_ref, send_ref = refs[0:2]
    stay_refs, go_refs = refs[2:4], refs[4:6]
    js_ref, joint_acc, mixing_acc = refs[6:9]
    z, y = me_ref[0], me_ref[1]
    attend_back_tree(
        (b0_ref, b1_ref), w_ref, qkv_ref, cos_ref, sin_ref, mask_ref, keep_ref, send_ref, js_ref
    )
    joint_acc[...] = dot(n0_ref[...], other_js[...], (0, 0)) + dot(n1_ref[...], js_ref[...], (0, 0))
    mixing_acc[...] = (
        dot(other0_ref[...], mixed0_ref[0:256, :], (0, 0))
        + dot(other1_ref[...], mixed0_ref[256:512, :], (0, 0))
        + dot(b0_ref[...], mixed1_ref[0:256, :], (0, 0))
        + dot(b1_ref[...], mixed1_ref[256:512, :], (0, 0))
    )
    for stream in range(2):
        order = stream_order(stream)
        for i in range(4):
            for j in range(4):
                dz, dy = (order[i], order[j]) if stream == 0 else (order[j], order[i])
                first = ((z ^ dz) * 4 + (y ^ dy)) * 128 + stream * 64
                rows = pl.ds(pl.multiple_of(first, 64), 64)
                out = stay_refs[stream] if i < 2 else go_refs[stream]
                out[i % 2, j, :, 0:512] = joint_acc[rows, :].astype(bf16)
                out[i % 2, j, :, 512:768] = mixing_acc[rows, :].astype(bf16)


def attend_back(me, branch, weights, qkv, cosine, sine, mask, tree, others=None):
    table = lambda width: pl.BlockSpec(
        (1, 512, width), lambda i, me: (tree, 0, 0), pipeline_mode=ONCE
    )
    part = ((256, 2048), bf16)
    shapes = [part, part]
    scratch = []
    if others is None:
        shapes.append(((512, 512), bf16))
    else:
        shapes += [((2, 4, 64, 768), bf16)] * 4
        scratch = [
            pltpu.VMEM((512, 512), bf16), pltpu.VMEM((2048, 512), f32), pltpu.VMEM((2048, 256), f32)
        ]
    extra = () if others is None else others
    return pl.pallas_call(
        attend_back_first_kernel if others is None else attend_back_second_kernel,
        grid_spec=pltpu.PrefetchScalarGridSpec(
            num_scalar_prefetch=1,
            grid=(1,),
            in_specs=[whole((256, 2048))] * 2 + [ATTEND_COLUMNS, whole((512, 512))]
            + [table(HD), table(HD), table(512)]
            + [whole(item.shape) for item in extra],
            out_specs=[whole(shape) for shape, _ in shapes],
            scratch_shapes=scratch,
        ),
        out_shape=[jax.ShapeDtypeStruct(shape, kind) for shape, kind in shapes],
        compiler_params=pltpu.CompilerParams(vmem_limit_bytes=(36 if others is None else 48) * MIB),
        cost_estimate=COST,
    )(me, *branch, weights, qkv, cosine, sine, mask, *extra)


SLOPE_CHUNKS = [pl.BlockSpec((128, 2048), lambda j, k=k: (k, 0)) for k in (1, 3)] * 2


def hidden_slope_kernel(*refs):
    x_refs, w_ref, o_ref, whole_ref = refs[:8], refs[8], refs[9], refs[10]

    @pl.when(pl.program_id(0) == 0)
    def _():
        for k in range(8):
            whole_ref[k * 128 : k * 128 + 128, :] = x_refs[k][...]

    o_ref[...] = dot(whole_ref[...], w_ref[...], (1, 0))


def hidden_slopes(feed0, feed1, weights):
    return pl.pallas_call(
        hidden_slope_kernel,
        grid=(4,),
        in_specs=SLOPE_CHUNKS * 2 + [pl.BlockSpec((2048, 256), lambda j: (0, j + 3))],
        out_specs=pl.BlockSpec((1024, 256), lambda j: (0, j)),
        out_shape=jax.ShapeDtypeStruct((1024, 1024), f32),
        scratch_shapes=[pltpu.VMEM((1024, 2048), bf16)],
        compiler_params=pltpu.CompilerParams(vmem_limit_bytes=48 * MIB),
        cost_estimate=COST,
    )(*rows_of(*feed0), *rows_of(*feed1), weights)


def feed_kernel(*refs):
    n_refs, gate_ref, up_ref, slope_ref, out0_ref, out1_ref, whole_ref = refs[:4], *refs[4:]

    @pl.when(pl.program_id(0) == 0)
    def _():
        for k in range(4):
            whole_ref[k * 256 : k * 256 + 256, :] = n_refs[k][...]

    for tree, out_ref in enumerate((out0_ref, out1_ref)):
        rows = slice(tree * 512, tree * 512 + 512)
        gate = dot(whole_ref[rows, :], gate_ref[...], (1, 0))
        upper = dot(whole_ref[rows, :], up_ref[...], (1, 0))
        slope = slope_ref[tree * 512 : tree * 512 + 512, :]
        sigma = jax.nn.sigmoid(gate)
        active = gate * sigma
        out_ref[0] = (slope * upper * sigma * (1.0 + gate * (1.0 - sigma))).astype(bf16)
        out_ref[1] = (slope * active).astype(bf16)
        out_ref[2] = (active * upper).astype(bf16)


def feed_forward(normed, weights, slopes):
    return pl.pallas_call(
        feed_kernel,
        grid=(4,),
        in_specs=[pl.BlockSpec((256, 2048), lambda j: (0, 0))] * 4
        + [
            pl.BlockSpec((2048, 256), lambda j: (0, j)),
            pl.BlockSpec((2048, 256), lambda j: (0, j + 4)),
            pl.BlockSpec((1024, 256), lambda j: (0, j)),
        ],
        out_specs=[pl.BlockSpec((3, 512, 256), lambda j: (0, 0, j))] * 2,
        out_shape=(jax.ShapeDtypeStruct((3, 512, 1024), bf16),) * 2,
        scratch_shapes=[pltpu.VMEM((1024, 2048), bf16)],
        compiler_params=pltpu.CompilerParams(vmem_limit_bytes=48 * MIB),
        cost_estimate=COST,
    )(*normed, weights, weights, slopes)


def feed_grad_kernel(*refs):
    n_refs, f_refs = refs[0:4], refs[4:12]
    s0_ref, s1_ref, out_ref, turned = refs[12:16]
    step = pl.program_id(0)

    @pl.when(step == 0)
    def _():
        for k in range(4):
            turned[:, k * 256 : k * 256 + 256] = n_refs[k][...].T

    @pl.when(step == 8)
    def _():
        for k in range(8):
            turned[:, k * 128 : k * 128 + 128] = f_refs[k][...].T

    slopes = jnp.concatenate([s0_ref[0], s1_ref[0]], axis=0)
    out_ref[...] = dot(turned[...], slopes, (1, 0)).astype(bf16)


def feed_grads(normed, feed0, feed1, slopes):
    return pl.pallas_call(
        feed_grad_kernel,
        grid=(12,),
        in_specs=[pl.BlockSpec((256, 2048), lambda j: (0, 0))] * 4
        + SLOPE_CHUNKS * 2
        + [pl.BlockSpec((1, 512, 256), lambda j: (j // 4, 0, j % 4))] * 2,
        out_specs=pl.BlockSpec((2048, 256), lambda j: (0, j)),
        out_shape=jax.ShapeDtypeStruct((2048, 3072), bf16),
        scratch_shapes=[pltpu.VMEM((2048, 1024), bf16)],
        compiler_params=pltpu.CompilerParams(vmem_limit_bytes=48 * MIB),
        cost_estimate=COST,
    )(*normed, *rows_of(*feed0), *rows_of(*feed1), *slopes)


def split_rows(part, keep_ref, send_ref):
    keep_ref[...] = part[0:256]
    send_ref[...] = part[256:512]


def normed_slope_kernel(g_ref, u_ref, wg_ref, wu_ref, keep_ref, send_ref):
    part = dot(g_ref[0], wg_ref[...], (1, 1)) + dot(u_ref[0], wu_ref[...], (1, 1))
    split_rows(part.astype(bf16), keep_ref, send_ref)


def normed_slopes(slopes, weights, tree):
    half = jax.ShapeDtypeStruct((256, 2048), bf16)
    return pl.pallas_call(
        normed_slope_kernel,
        grid=(4,),
        in_specs=[
            pl.BlockSpec((1, 512, 1024), lambda j: (0, 0, 0), pipeline_mode=ONCE),
            pl.BlockSpec((1, 512, 1024), lambda j: (1, 0, 0), pipeline_mode=ONCE),
            pl.BlockSpec((512, 1024), lambda j: (j, 0)),
            pl.BlockSpec((512, 1024), lambda j: (j, 1)),
        ],
        out_specs=[pl.BlockSpec((256, 512), lambda j: (0, j))] * 2,
        out_shape=(half, half),
        compiler_params=pltpu.CompilerParams(vmem_limit_bytes=(20 if tree else 48) * MIB),
        cost_estimate=COST,
    )(slopes, slopes, weights, weights)


def down_kernel(h_ref, w0, w1, w2, w3, keep_ref, send_ref):
    weights = jnp.concatenate([w0[...], w1[...], w2[...], w3[...]], axis=1)
    split_rows(dot(h_ref[0], weights, (1, 1)).astype(bf16), keep_ref, send_ref)


def down(slopes, weights):
    half = jax.ShapeDtypeStruct((256, 2048), bf16)
    return pl.pallas_call(
        down_kernel,
        grid=(4,),
        in_specs=[
            pl.BlockSpec((1, 512, 1024), lambda j: (2, 0, 0)),
            pl.BlockSpec((512, 256), lambda j: (j, 3)),
            pl.BlockSpec((512, 256), lambda j: (j, 4)),
            pl.BlockSpec((512, 256), lambda j: (j, 5)),
            pl.BlockSpec((512, 256), lambda j: (j, 6)),
        ],
        out_specs=[pl.BlockSpec((256, 512), lambda j: (0, j))] * 2,
        out_shape=(half, half),
        compiler_params=pltpu.CompilerParams(vmem_limit_bytes=48 * MIB),
        cost_estimate=COST,
    )(slopes, *([weights] * 4))


def norm_back(slope, incoming, scale, gain):
    weighted = slope * gain
    cubed = scale * scale * scale
    return scale * weighted - incoming * cubed * jnp.mean(weighted * incoming, axis=1, keepdims=True)


def shards(
    tokens, attend_gain, joint_weight, mixing_weight, feed_gain, gate_weight, up_weight,
    down_weight, lengths, parents, cotangent,
):
    z, y = lax.axis_index("z"), lax.axis_index("y")
    xh, xl, core = lax.axis_index("xh"), lax.axis_index("xl"), lax.axis_index("core")
    me = jnp.stack([z, y, xh * 4 + xl * 2 + core, xh]).astype(jnp.int32)

    def home_start(total):
        rows = total.shape[0] // 2
        own = jnp.where(xh == 0, total[:rows], total[rows:])
        return own, team_swap(jnp.where(xh == 0, total[rows:], total[:rows]), 1, 0, 0)

    def home_end(own, other, widths):
        first = jnp.where(xh == 0, own, other).astype(f32)
        second = jnp.where(xh == 0, other, own).astype(f32)
        out, at = [], 0
        for width in widths:
            out.append(
                jnp.concatenate([first[:, at : at + width], second[:, at : at + width]], axis=1)
            )
            at += width
        return out

    gains = jnp.concatenate([attend_gain, feed_gain])[None]
    own, send = prepare_weights(
        prepare_attend_kernel, me, 1920, joint_weight, mixing_weight.T, down_weight.T, gains
    )
    other = team_swap(send, 1, 0, 0)
    trees = jnp.concatenate([lengths, parents], axis=0)
    other, trees_other = after((other, team_swap(trees, 1, 0, 0)))
    own_rows, cotangent_own = prepare_rows(tokens[:, 0], after(cotangent[:, 0], send))
    attend_rows = place_rows(me, own, other)
    weights = lax.all_gather(attend_rows, GRID, axis=0, tiled=True)

    rows_started = gather_start(after(own_rows, attend_rows))
    feed_stay, feed_send = prepare_weights(
        prepare_feed_kernel, me, 2048, gate_weight, after(up_weight, attend_rows)
    )
    trees = jnp.stack([trees, trees_other])
    chunk = jnp.arange(4, dtype=jnp.int32)
    place = ((xl ^ (chunk % 2)) * 2 + (core ^ (chunk // 2))) * 128
    place = (place[:, None] + jnp.arange(128, dtype=jnp.int32)[None]).reshape(512)
    position, mask = tree_tables(trees[:, 0], trees[:, 1], place)
    cosine, sine = rotary_tables(position)
    rows_started, mask, cosine, sine, feed_send = after(
        (rows_started, mask, cosine, sine, feed_send)
    )
    rows_later = gather_next(own_rows, rows_started)
    feed_other = team_swap(feed_send, 1, 0, 0)
    rows_later, feed_other = after((rows_later, feed_other))
    feed_rows = place_rows(me, feed_stay, feed_other)
    feed_weights = lax.all_gather(feed_rows, GRID, axis=0, tiled=True)
    rows0 = gather_first(rows_later)
    rows1 = gather_second(rows_started, rows_later)
    rows0, rows1, feed_rows, weights = after((rows0, rows1, feed_rows, weights))

    gains, normed1, qkv1, mixed1, *part1 = attend(me, rows1, weights, cosine, sine, mask, 1)
    sums1 = scatter_sums(scatter_start(part1), 1)
    terms1 = scatter_next(sums1, 1)
    _, normed0, qkv0, mixed0, *part0 = attend(
        me, after(rows0, sums1), weights, cosine, sine, mask, 0
    )
    sums0 = scatter_sums(scatter_start(part0), 0)
    terms0 = scatter_next(sums0, 0)
    hidden_slope = hidden_slopes(after(rows0, sums0), rows1, weights)
    terms0, terms1, hidden_slope = after((terms0, terms1, hidden_slope))
    gain_one, gain_two = gains[0:1], gains[1:2]
    incoming = own_rows[:128].astype(f32)
    middle = incoming + total(terms0 + terms1)
    scale_two = lax.rsqrt(jnp.mean(middle * middle, axis=1, keepdims=True) + EPSILON)
    low = (middle * scale_two * gain_two).astype(bf16)
    started = gather_start(low)
    later = gather_next(low, started)
    two = gather_first(later) + gather_second(started, later)

    slopes0, slopes1 = feed_forward(two, feed_weights, hidden_slope)
    sums1 = scatter_sums(scatter_start(normed_slopes(slopes1, feed_weights, 1)), 1)
    terms1 = scatter_next(sums1, 1)
    feed_grad = feed_grads(two, rows0, rows1, after((slopes0, slopes1), sums1))
    terms1, feed_grad = after((terms1, feed_grad))
    feed_sum = lax.psum_scatter(feed_grad, GRID, scatter_dimension=0, tiled=True)
    sums0 = scatter_sums(scatter_start(normed_slopes(after(slopes0, feed_grad), feed_weights, 0)), 0)
    terms0 = scatter_next(sums0, 0)
    down0 = down(after(slopes0, sums0), weights)
    down1 = down(after(slopes1, sums0), weights)
    terms0, down0, down1 = after((terms0, down0, down1))

    middle_slope = cotangent_own + norm_back(
        total(terms0 + terms1), middle, scale_two, gain_two
    )
    low = middle_slope.astype(bf16)
    started = gather_start(low)
    down0, down1 = after((down0, down1), low)
    down0 = scatter_sums(scatter_start(down0), 0)
    down1 = scatter_sums(scatter_start(down1), 1)
    started, down0, down1 = after((started, down0, down1))
    later = gather_next(low, started)
    branch0 = gather_first(later)
    keep0, send0, js0 = attend_back(me, branch0, weights, qkv0, cosine, sine, mask, 0)
    branch1 = gather_second(started, later)

    sums0 = scatter_sums(scatter_start((keep0, send0)), 0)
    input_terms0 = scatter_next(sums0, 0)
    down_terms = scatter_next(down0, 0) + scatter_next(down1, 1)
    keep1, send1, *streams = attend_back(
        me, after(branch1, js0, sums0, down0, down1), weights, qkv1, cosine, sine, mask, 1,
        (*branch0, js0, normed0, normed1, mixed0, mixed1),
    )
    keep1, send1, down_terms = after((keep1, send1, down_terms))

    input_terms1 = scatter_next(scatter_sums(scatter_start((keep1, send1)), 1), 1)
    feed_own, feed_other = home_start(feed_sum)
    attend_sum, (input_terms0, input_terms1), feed_other = grid_scatter(
        streams[:2], streams[2:], (input_terms0, input_terms1), feed_other
    )
    layer_output = middle + total(down_terms)
    attend_own, attend_other = home_start(attend_sum)
    scale_one = lax.rsqrt(jnp.mean(incoming * incoming, axis=1, keepdims=True) + EPSILON)
    input_gradient = middle_slope + norm_back(
        total(input_terms0 + input_terms1), incoming, scale_one, gain_one
    )
    gate_grad, up_grad, down_grad = home_end(feed_own, feed_other, (1024, 1024, 1024))
    joint_grad, mixing_grad = home_end(attend_own, attend_other, (512, 256))

    attend_part = jnp.sum(joint_weight.astype(f32) * joint_grad, axis=1)
    feed_part = jnp.sum(
        gate_weight.astype(f32) * gate_grad + up_weight.astype(f32) * up_grad, axis=1
    )
    attend_total, feed_total = lax.psum((attend_part, feed_part), ("xl", "core"))
    return (
        lane_back(layer_output)[:, None],
        lane_back(input_gradient)[:, None],
        attend_total / attend_gain.astype(f32),
        joint_grad,
        mixing_grad.T,
        feed_total / feed_gain.astype(f32),
        gate_grad,
        up_grad,
        down_grad.T,
    )


def solution(mesh):
    fine = Mesh(mesh.devices.reshape(4, 2, 4, 2, 2), ("z", "xh", "y", "xl", "core"))
    fsdp = ("z", "xh", "y")
    tensor = ("xl", "core")
    in_specs = (
        P(tensor, fsdp, None),
        P(fsdp),
        P(fsdp, tensor),
        P(tensor, fsdp),
        P(fsdp),
        P(fsdp, tensor),
        P(fsdp, tensor),
        P(tensor, fsdp),
        P(fsdp, None),
        P(fsdp, None),
        P(tensor, fsdp, None),
    )
    out_specs = (
        P(tensor, fsdp, None),
        P(tensor, fsdp, None),
        P(fsdp),
        P(fsdp, tensor),
        P(tensor, fsdp),
        P(fsdp),
        P(fsdp, tensor),
        P(fsdp, tensor),
        P(tensor, fsdp),
    )
    return jax.shard_map(shards, mesh=fine, in_specs=in_specs, out_specs=out_specs, check_vma=False)
```
